256 devices in a mesh: pipe: 4 (over z_lo, core), vocab: 64 (over x, y, z_hi).
Axes of the slice: x: 4, y: 4, z: 8 (z_hi: 4, z_lo: 2; z = z_hi * 2 + z_lo), core: 2. Of those that a mesh axis runs over, the one named last changes fastest.
Arguments:
- student_hidden: bfloat16 [512, 5120], P('pipe', 'vocab'), may hold values from -30 to 30
- teacher_hidden: bfloat16 [512, 4096], P('pipe', 'vocab'), may hold values from -30 to 30
- student_head: bfloat16 [98304, 5120], P(('pipe', 'vocab')), may hold values from -3 to 3
- teacher_head: bfloat16 [98304, 4096], P(('pipe', 'vocab')), may hold values from -3 to 3
- row_weight: float32 [512], replicated, may hold values from 2 to 16
Outputs:
- kl_rows: float32 [512], P('pipe')
- hidden_grad: float32 [512, 5120], P('pipe', 'vocab')
- head_grad: bfloat16 [98304, 5120], P(('pipe', 'vocab'))
The draws below stay inside these ranges and needn't reach their ends.
All inputs are finite; a program needn't handle non-finite values.
Results may differ from the reference program's by a relative error of at most 0.017.
Values may be sent and summed in bfloat16 or wider, within the bound.
No kernel may reach another device: no remote copies, remote signals or barrier semaphores. Data moves between devices by JAX's collectives and lax.ppermute only.
A program may use at most 128 MiB of HBM per device.

```python
import math
import jax
import jax.numpy as jnp
from jax import lax

DS = 5120
DT = 4096
TOKENS = 512
VOCAB = 98304


def head_rows(key, row_ids, columns, salt_value, spread):
    base_key = jax.random.fold_in(key, salt_value)
    common_key = jax.random.fold_in(key, salt_value + 1000)
    common = jnp.clip(jax.random.normal(common_key, (columns,), jnp.float32), -6.0, 6.0) * (3.0 / jnp.sqrt(float(columns)))

    def one_row(row_index):
        row_key = jax.random.fold_in(base_key, row_index)
        noise_key, scale_key = jax.random.split(row_key)
        values = jnp.clip(jax.random.normal(noise_key, (columns,), jnp.float32), -6.0, 6.0)
        factor = jnp.exp(jax.random.uniform(scale_key, (), jnp.float32) * jnp.log(spread))
        rising = 1.0 + 0.5 * row_index.astype(jnp.float32) / float(VOCAB)
        return values * (3.0 / jnp.sqrt(float(columns))) * factor * rising + common
    return jax.vmap(one_row)(row_ids)


def hidden_rows(key, own_salt, columns):
    own_key = jax.random.fold_in(key, own_salt)
    base_key, scale_key = jax.random.split(own_key, 2)
    values = jnp.clip(jax.random.normal(base_key, (TOKENS, columns), jnp.float32), -6.0, 6.0)
    scales = jnp.exp(jax.random.uniform(scale_key, (TOKENS, 1), jnp.float32, jnp.log(0.06), jnp.log(0.3)))
    values = values * scales
    return values


def draw_student_hidden(key, part):
    return hidden_rows(key, 5, DS).astype(jnp.bfloat16)


def draw_teacher_hidden(key, part):
    return hidden_rows(key, 6, DT).astype(jnp.bfloat16)


def draw_student_head(key, part):
    spread = 2.0
    return head_rows(key, jnp.arange(VOCAB, dtype=jnp.int32), DS, 101, spread).astype(jnp.bfloat16)


def draw_teacher_head(key, part):
    spread = 2.0
    return head_rows(key, jnp.arange(VOCAB, dtype=jnp.int32), DT, 102, spread).astype(jnp.bfloat16)


def setup_inputs(seed: int = 0) -> dict:
    splits = jax.random.split(jax.random.key(seed), 6)
    return {
        "student_hidden": draw_student_hidden(jax.random.fold_in(splits[5], 71), 0),
        "teacher_hidden": draw_teacher_hidden(jax.random.fold_in(splits[5], 71), 0),
        "student_head": draw_student_head(jax.random.fold_in(splits[5], 71), 0),
        "teacher_head": draw_teacher_head(jax.random.fold_in(splits[5], 71), 0),
        "row_weight": jnp.clip(jnp.exp(jax.random.uniform(splits[4], (TOKENS,), jnp.float32, math.log(2.0), math.log(16.0))), 2.0, 16.0),
    }


def dot_rows(left, right):
    return lax.dot_general(left, right, (((1,), (1,)), ((), ())), preferred_element_type=jnp.float32)


def reference(student_hidden, teacher_hidden, student_head, teacher_head, row_weight):
    student_logits = dot_rows(student_hidden, student_head)
    teacher_logits = dot_rows(teacher_hidden, teacher_head)
    student_max = jnp.max(student_logits, axis=1)
    teacher_max = jnp.max(teacher_logits, axis=1)
    student_exp = jnp.exp(student_logits - student_max[:, None])
    teacher_exp = jnp.exp(teacher_logits - teacher_max[:, None])
    student_total = jnp.sum(student_exp, axis=1)
    teacher_total = jnp.sum(teacher_exp, axis=1)
    cross = jnp.sum(teacher_exp * (teacher_logits - student_logits), axis=1)
    kl_rows = cross / teacher_total - teacher_max - jnp.log(teacher_total) + student_max + jnp.log(student_total)
    logit_grad = (row_weight[:, None] * (student_exp / student_total[:, None] - teacher_exp / teacher_total[:, None])).astype(jnp.bfloat16)
    hidden_grad = jnp.dot(logit_grad, student_head, preferred_element_type=jnp.float32)
    head_grad = lax.dot_general(logit_grad, student_hidden, (((0,), (0,)), ((), ())), preferred_element_type=jnp.float32).astype(jnp.bfloat16)
    return kl_rows, hidden_grad, head_grad
```

```python
import jax
import jax.numpy as jnp
from jax import lax
from jax.experimental import pallas as pl
from jax.experimental.pallas import tpu as pltpu
from jax.sharding import PartitionSpec as P

DS, DT = 5120, 4096
ROWS = 384
TOK = 256
NS, NT = 320, 256
AXES = ("pipe", "vocab")
F32, BF16 = jnp.float32, jnp.bfloat16
VMEM_LIMIT = 48 * 1024 * 1024


def coords(i):
    p, v = divmod(i, 64)
    return p >> 1, p & 1, v >> 4, (v >> 2) & 3, v & 3


def index(zl, c, x, y, zh):
    return (zl * 2 + c) * 64 + x * 16 + y * 4 + zh


def perm(move):
    return [(i, index(*move(*coords(i)))) for i in range(256)]


PAIR = perm(lambda zl, c, x, y, zh: (1 - zl, c, x, y, zh))
CORE = perm(lambda zl, c, x, y, zh: (zl, 1 - c, x, y, zh))
ZH = {k: perm(lambda zl, c, x, y, zh, k=k: (zl, c, x, y, (zh + k) % 4)) for k in (1, 2, 3)}
FIRST = {
    k: perm(lambda zl, c, x, y, zh, k=k: (zl, c, (x + k * (1 - c)) % 4, (y + k * c) % 4, zh))
    for k in (1, 2, 3)
}
SECOND = {
    k: perm(lambda zl, c, x, y, zh, k=k: (zl, c, (x + k * c) % 4, (y + k * (1 - c)) % 4, zh))
    for k in (1, 2, 3)
}


def send(value, pairs):
    return lax.ppermute(value, AXES, pairs)


def ring(value, perms):
    got = {k: send(value, perms[k]) for k in (1, 3, 2)}
    return got[1], got[2], got[3]


def place():
    p, v = lax.axis_index("pipe"), lax.axis_index("vocab")
    return p >> 1, p & 1, v >> 4, (v >> 2) & 3, v & 3


def block_at(c, x, y, first, second):
    in_x = jnp.where(c == 0, first, second)
    in_y = jnp.where(c == 0, second, first)
    return ((x + in_x) & 3) * 4 + ((y + in_y) & 3)


def dot(a, b, dims):
    return lax.dot_general(a, b, (dims, ((), ())), preferred_element_type=F32)


def logits_kernel(
    t0, t1, t2, t3, ws, wso, wt, wto, es_ref, et_ref, st_ref, hs_out, hs, ht, wsb, wtb, hsem, wsem, osem
):
    _, c, x, y, _ = place()
    copies_t, copies_s = [], []
    for j, t in enumerate((t0, t1, t2, t3)):
        for i in range(4):
            at = block_at(c, x, y, (4 - i) & 3, (4 - j) & 3)
            n = (j * 4 + i) * 2
            copies_t.append(
                pltpu.make_async_copy(
                    t.at[i, pl.ds(NS, NT)],
                    ht.at[pl.ds(pl.multiple_of(at * NT, NT), NT)],
                    hsem.at[n],
                )
            )
            copies_s.append(
                pltpu.make_async_copy(
                    t.at[i, pl.ds(0, NS)],
                    hs.at[pl.ds(pl.multiple_of(at * NS, NS), NS)],
                    hsem.at[n + 1],
                )
            )
    weights = [
        pltpu.make_async_copy(src, dst.at[pl.ds(half * ROWS, ROWS)], wsem.at[n])
        for n, (src, dst, half) in enumerate(
            ((wt, wtb, 0), (wto, wtb, 1), (ws, wsb, 0), (wso, wsb, 1))
        )
    ]
    for copy in copies_t + weights[:2] + copies_s + weights[2:]:
        copy.start()
    for copy in copies_t:
        copy.wait()
    for half in range(2):
        weights[half].wait()
        rows = pl.ds(half * ROWS, ROWS)
        et_ref[rows] = dot(wtb[rows], ht[...], ((1,), (0,)))
    for copy in copies_s:
        copy.wait()
    out = pltpu.make_async_copy(hs, hs_out, osem)
    out.start()
    for half in range(2):
        weights[2 + half].wait()
        rows = pl.ds(half * ROWS, ROWS)
        es_ref[rows] = dot(wsb[rows], hs[...], ((1,), (0,)))
    s, t = es_ref[...], et_ref[...]
    sm = jnp.max(s, axis=0, keepdims=True)
    tm = jnp.max(t, axis=0, keepdims=True)
    es, et = jnp.exp(s - sm), jnp.exp(t - tm)
    st_ref[0:1] = sm
    st_ref[1:2] = tm
    st_ref[2:3] = jnp.sum(es, axis=0, keepdims=True)
    st_ref[3:4] = jnp.sum(et, axis=0, keepdims=True)
    st_ref[4:5] = jnp.sum(et * (t - s), axis=0, keepdims=True)
    st_ref[5:8] = jnp.zeros((3, TOK), F32)
    es_ref[...] = es
    et_ref[...] = et
    out.wait()


def logits_call(parts, ws, wso, wt, wto):
    hbm = pl.BlockSpec(memory_space=pl.ANY)
    vmem = pl.BlockSpec(memory_space=pltpu.VMEM)
    return pl.pallas_call(
        logits_kernel,
        out_shape=(
            jax.ShapeDtypeStruct((2 * ROWS, TOK), F32),
            jax.ShapeDtypeStruct((2 * ROWS, TOK), F32),
            jax.ShapeDtypeStruct((8, TOK), F32),
            jax.ShapeDtypeStruct((DS, TOK), BF16),
        ),
        in_specs=[hbm] * 8,
        out_specs=(vmem, vmem, vmem, hbm),
        scratch_shapes=[
            pltpu.VMEM((DS, TOK), BF16),
            pltpu.VMEM((DT, TOK), BF16),
            pltpu.VMEM((2 * ROWS, DS), BF16),
            pltpu.VMEM((2 * ROWS, DT), BF16),
            pltpu.SemaphoreType.DMA((32,)),
            pltpu.SemaphoreType.DMA((4,)),
            pltpu.SemaphoreType.DMA,
        ],
        compiler_params=pltpu.CompilerParams(vmem_limit_bytes=VMEM_LIMIT),
        cost_estimate=pl.CostEstimate(
            flops=2 * 2 * ROWS * TOK * (DS + DT), bytes_accessed=22_000_000, transcendentals=4 * ROWS * TOK
        ),
        name="logits",
    )(*parts, ws, wso, wt, wto)


CHUNK = 1280


def grads_kernel(
    es_ref, et_ref, coef_ref, ws, wso, g_own, g_oth, o0, o1, o2, o3, wsb, acc, accb, wsem, osem
):
    _, c, x, y, _ = place()
    weights = []
    for n in range(DS // CHUNK):
        for half, src in enumerate((ws, wso)):
            cols = pl.ds(n * CHUNK, CHUNK)
            weights.append(
                pltpu.make_async_copy(
                    src.at[:, cols], wsb.at[pl.ds(half * ROWS, ROWS), cols], wsem.at[2 * n + half]
                )
            )
    for copy in weights:
        copy.start()
    g = (es_ref[...] * coef_ref[0:1] - et_ref[...] * coef_ref[1:2]).astype(BF16)
    g_own[...] = g[:ROWS]
    g_oth[...] = g[ROWS:]
    for n in range(DS // CHUNK):
        weights[2 * n].wait()
        weights[2 * n + 1].wait()
        part = dot(wsb[:, n * CHUNK : (n + 1) * CHUNK], g, ((0,), (0,)))
        acc[n * CHUNK : (n + 1) * CHUNK] = part
        accb[n * CHUNK : (n + 1) * CHUNK] = part.astype(BF16)
    outs = []
    for k, o in ((1, o1), (3, o3), (2, o2), (0, o0)):
        for r in range(4):
            at = block_at(c, x, y, r, k)
            src = acc if k == 0 else accb
            outs.append(
                pltpu.make_async_copy(
                    src.at[pl.ds(pl.multiple_of(at * NS, NS), NS)], o.at[r], osem.at[k * 4 + r]
                )
            )
    for copy in outs:
        copy.start()
    for copy in outs:
        copy.wait()


def grads_call(es, et, coef, ws, wso):
    hbm = pl.BlockSpec(memory_space=pl.ANY)
    vmem = pl.BlockSpec(memory_space=pltpu.VMEM)
    piece = (4, NS, TOK)
    return pl.pallas_call(
        grads_kernel,
        out_shape=(
            jax.ShapeDtypeStruct((ROWS, TOK), BF16),
            jax.ShapeDtypeStruct((ROWS, TOK), BF16),
            jax.ShapeDtypeStruct(piece, F32),
            jax.ShapeDtypeStruct(piece, BF16),
            jax.ShapeDtypeStruct(piece, BF16),
            jax.ShapeDtypeStruct(piece, BF16),
        ),
        in_specs=[vmem, vmem, vmem, hbm, hbm],
        out_specs=(vmem, vmem, hbm, hbm, hbm, hbm),
        scratch_shapes=[
            pltpu.VMEM((2 * ROWS, DS), BF16),
            pltpu.VMEM((DS, TOK), F32),
            pltpu.VMEM((DS, TOK), BF16),
            pltpu.SemaphoreType.DMA((8,)),
            pltpu.SemaphoreType.DMA((16,)),
        ],
        compiler_params=pltpu.CompilerParams(vmem_limit_bytes=VMEM_LIMIT),
        cost_estimate=pl.CostEstimate(
            flops=2 * 2 * ROWS * TOK * DS, bytes_accessed=14_000_000, transcendentals=0
        ),
        name="grads",
    )(es, et, coef, ws, wso)


def head_kernel(g_own, g_got, h_own, h_got, out):
    out[...] = (
        dot(g_own[...], h_own[...], ((1,), (1,))) + dot(g_got[...], h_got[...], ((1,), (1,)))
    ).astype(BF16)


def head_call(g_own, g_got, h_own, h_got):
    step = 640
    whole = pl.BlockSpec((ROWS, TOK), lambda i: (0, 0))
    some = pl.BlockSpec((step, TOK), lambda i: (i, 0))
    return pl.pallas_call(
        head_kernel,
        out_shape=jax.ShapeDtypeStruct((ROWS, DS), BF16),
        grid=(DS // step,),
        in_specs=[whole, whole, some, some],
        out_specs=pl.BlockSpec((ROWS, step), lambda i: (0, i)),
        compiler_params=pltpu.CompilerParams(vmem_limit_bytes=VMEM_LIMIT),
        cost_estimate=pl.CostEstimate(
            flops=2 * 2 * ROWS * TOK * DS, bytes_accessed=10_000_000, transcendentals=0
        ),
        name="head",
    )(g_own, g_got, h_own, h_got)


def merge(stats):
    top = stats[0][0:2]
    for s in stats[1:]:
        top = jnp.maximum(top, s[0:2])
    total = jnp.zeros_like(stats[0][2:5])
    for s in stats:
        scale = jnp.exp(s[0:2] - top)
        total = total + s[2:5] * jnp.concatenate([scale, scale[1:2]], axis=0)
    return jnp.concatenate([top, total, stats[0][5:8]], axis=0)


def per_device(student_hidden, teacher_hidden, student_head, teacher_head, row_weight):
    zl, c, x, y, zh = place()

    teacher_other = send(teacher_head, CORE)
    student_other = send(student_head, CORE)

    mine = jnp.concatenate([student_hidden.T, teacher_hidden.T], axis=0)
    pair = send(mine, PAIR)
    both = jnp.concatenate(
        [jnp.where(zl == 0, mine, pair), jnp.where(zl == 0, pair, mine)], axis=1
    )
    around = (both,) + ring(both, ZH)
    ordered = [lax.select_n((zh - q) & 3, *around) for q in range(4)]
    block = jnp.concatenate([o[:80] for o in ordered] + [o[80:] for o in ordered], axis=0)
    line = jnp.stack((block,) + ring(block, FIRST))
    parts = (line,) + ring(line, SECOND)

    es, et, local, hidden_own = logits_call(
        parts, student_head, student_other, teacher_head, teacher_other
    )
    hidden_got = send(hidden_own, CORE)

    stats = merge((local, send(local, PAIR)))
    for perms in (ZH, FIRST, SECOND):
        stats = merge((stats,) + ring(stats, perms))
    student_max, teacher_max, student_total, teacher_total, cross = (stats[i] for i in range(5))
    kl_both = (
        cross / teacher_total
        - teacher_max
        - jnp.log(teacher_total)
        + student_max
        + jnp.log(student_total)
    )
    kl_rows = lax.dynamic_slice_in_dim(kl_both, zl * 128, 128, 0)
    weight = lax.dynamic_index_in_dim(row_weight.reshape(2, 2, 128), c, 1, False).reshape(TOK)
    coef = jnp.stack(
        [
            weight * (jnp.exp(local[0] - student_max) / student_total),
            weight * (jnp.exp(local[1] - teacher_max) / teacher_total),
        ]
    )
    coef = jnp.concatenate([coef, jnp.zeros((6, TOK), F32)], axis=0)

    g_own, g_oth, o0, o1, o2, o3 = grads_call(es, et, coef, student_head, student_other)
    g_got = send(g_oth, CORE)
    r1, r3, r2 = send(o1, SECOND[1]), send(o3, SECOND[3]), send(o2, SECOND[2])
    head_grad = head_call(g_own, g_got, hidden_own, hidden_got)

    sums = o0 + (r1.astype(F32) + r3.astype(F32)) + r2.astype(F32)
    r1, r3, r2 = (send(sums[k].astype(BF16), FIRST[k]) for k in (1, 3, 2))
    sums = (sums[0] + (r1.astype(F32) + r3.astype(F32)) + r2.astype(F32)).reshape(4, 80, TOK)
    narrow = sums.astype(BF16)
    r1, r3, r2 = (
        send(lax.dynamic_index_in_dim(narrow, (zh + k) & 3, 0, False), ZH[k]) for k in (1, 3, 2)
    )
    sums = lax.dynamic_index_in_dim(sums, zh, 0, False) + (r1.astype(F32) + r3.astype(F32)) + r2.astype(F32)
    low, high = sums[:, :128], sums[:, 128:]
    got = send(jnp.where(zl == 0, high, low), PAIR)
    hidden_grad = (jnp.where(zl == 0, low, high) + got).T
    return (kl_rows, hidden_grad, head_grad)


def solution(mesh):
    placed = (
        P("pipe", "vocab"),
        P("pipe", "vocab"),
        P(("pipe", "vocab"), None),
        P(("pipe", "vocab"), None),
        P(),
    )
    return jax.shard_map(
        per_device,
        mesh=mesh,
        in_specs=placed,
        out_specs=(P("pipe"), P("pipe", "vocab"), P(("pipe", "vocab"), None)),
        check_vma=False,
    )
```

```python
import jax
import jax.numpy as jnp
from jax import lax
from jax.experimental import pallas as pl
from jax.experimental.pallas import tpu as pltpu
from jax.sharding import PartitionSpec as P

DS, DT = 5120, 4096
ROWS = 384
TOK = 256
NS, NT = 320, 256
AXES = ("pipe", "vocab")
F32, BF16 = jnp.float32, jnp.bfloat16
VMEM_LIMIT = 20 * 1024 * 1024


def coords(i):
    p, v = divmod(i, 64)
    return p >> 1, p & 1, v >> 4, (v >> 2) & 3, v & 3


def index(zl, c, x, y, zh):
    return (zl * 2 + c) * 64 + x * 16 + y * 4 + zh


def perm(move):
    return [(i, index(*move(*coords(i)))) for i in range(256)]


PAIR = perm(lambda zl, c, x, y, zh: (1 - zl, c, x, y, zh))
CORE = perm(lambda zl, c, x, y, zh: (zl, 1 - c, x, y, zh))
ZH = {k: perm(lambda zl, c, x, y, zh, k=k: (zl, c, x, y, (zh + k) % 4)) for k in (1, 2, 3)}
FIRST = {
    k: perm(lambda zl, c, x, y, zh, k=k: (zl, c, (x + k * (1 - c)) % 4, (y + k * c) % 4, zh))
    for k in (1, 2, 3)
}
SECOND = {
    k: perm(lambda zl, c, x, y, zh, k=k: (zl, c, (x + k * c) % 4, (y + k * (1 - c)) % 4, zh))
    for k in (1, 2, 3)
}


def send(value, pairs):
    return lax.ppermute(value, AXES, pairs)


def ring(value, perms):
    got = {k: send(value, perms[k]) for k in (1, 3, 2)}
    return got[1], got[2], got[3]


def place():
    p, v = lax.axis_index("pipe"), lax.axis_index("vocab")
    return p >> 1, p & 1, v >> 4, (v >> 2) & 3, v & 3


def block_at(c, x, y, first, second):
    in_x = jnp.where(c == 0, first, second)
    in_y = jnp.where(c == 0, second, first)
    return ((x + in_x) & 3) * 4 + ((y + in_y) & 3)


def dot(a, b, dims):
    return lax.dot_general(a, b, (dims, ((), ())), preferred_element_type=F32)


def logits_kernel(t0, t1, t3, t2a, t2b, ws, wso, wt, wto, es_ref, et_ref, st_ref, hs, ht):
    _, c, x, y, _ = place()
    parts = [(0, t0, 0, range(4)), (1, t1, 0, range(4)), (3, t3, 0, range(4))]
    parts += [(2, t2a, 0, range(2)), (2, t2b, 2, range(2, 4))]
    for j, t, base, lines in parts:
        for i in lines:
            at = block_at(c, x, y, (4 - i) & 3, (4 - j) & 3)
            ht[pl.ds(pl.multiple_of(at * NT, NT), NT)] = t[i - base, NS : NS + NT]
            hs[pl.ds(pl.multiple_of(at * NS, NS), NS)] = t[i - base, 0:NS]
    et_ref[:ROWS] = dot(wt[...], ht[...], ((1,), (0,)))
    et_ref[ROWS:] = dot(wto[...], ht[...], ((1,), (0,)))
    es_ref[:ROWS] = dot(ws[...], hs[...], ((1,), (0,)))
    es_ref[ROWS:] = dot(wso[...], hs[...], ((1,), (0,)))
    s, t = es_ref[...], et_ref[...]
    sm = jnp.max(s, axis=0, keepdims=True)
    tm = jnp.max(t, axis=0, keepdims=True)
    es, et = jnp.exp(s - sm), jnp.exp(t - tm)
    st_ref[0:1] = sm
    st_ref[1:2] = tm
    st_ref[2:3] = jnp.sum(es, axis=0, keepdims=True)
    st_ref[3:4] = jnp.sum(et, axis=0, keepdims=True)
    st_ref[4:5] = jnp.sum(et * (t - s), axis=0, keepdims=True)
    st_ref[5:8] = jnp.zeros((3, TOK), F32)
    es_ref[...] = es
    et_ref[...] = et


def logits_call(parts, ws, wso, wt, wto):
    vmem = pl.BlockSpec(memory_space=pltpu.VMEM)
    return pl.pallas_call(
        logits_kernel,
        out_shape=(
            jax.ShapeDtypeStruct((2 * ROWS, TOK), F32),
            jax.ShapeDtypeStruct((2 * ROWS, TOK), F32),
            jax.ShapeDtypeStruct((8, TOK), F32),
            jax.ShapeDtypeStruct((DS, TOK), BF16),
        ),
        in_specs=[vmem] * 9,
        out_specs=(vmem,) * 4,
        scratch_shapes=[pltpu.VMEM((DT, TOK), BF16)],
        compiler_params=pltpu.CompilerParams(vmem_limit_bytes=VMEM_LIMIT),
        cost_estimate=pl.CostEstimate(
            flops=2 * 2 * ROWS * TOK * (DS + DT), bytes_accessed=22_000_000, transcendentals=4 * ROWS * TOK
        ),
        name="logits",
    )(*parts, ws, wso, wt, wto)


CHUNK = 1280


def grads_kernel(es_ref, et_ref, coef_ref, ws, wso, g_own, g_oth, o0, o1, o3, o2a, o2b, acc):
    _, c, x, y, _ = place()
    g = (es_ref[...] * coef_ref[0:1] - et_ref[...] * coef_ref[1:2]).astype(BF16)
    g_own[...] = g[:ROWS]
    g_oth[...] = g[ROWS:]
    for n in range(DS // CHUNK):
        cols = slice(n * CHUNK, (n + 1) * CHUNK)
        part = dot(g[:ROWS], ws[:, cols], ((0,), (0,))) + dot(g[ROWS:], wso[:, cols], ((0,), (0,)))
        acc[cols] = part.astype(BF16).T
    outs = [(0, o0, 0, range(4)), (1, o1, 0, range(4)), (3, o3, 0, range(4))]
    outs += [(2, o2a, 0, range(2)), (2, o2b, 2, range(2, 4))]
    for k, o, base, lines in outs:
        for r in lines:
            at = block_at(c, x, y, r, k)
            o[r - base] = acc[pl.ds(pl.multiple_of(at * NS, NS), NS)]


def grads_call(es, et, coef, ws, wso):
    vmem = pl.BlockSpec(memory_space=pltpu.VMEM)
    whole = jax.ShapeDtypeStruct((4, NS, TOK), BF16)
    half = jax.ShapeDtypeStruct((2, NS, TOK), BF16)
    rows = jax.ShapeDtypeStruct((ROWS, TOK), BF16)
    return pl.pallas_call(
        grads_kernel,
        out_shape=(rows, rows, whole, whole, whole, half, half),
        in_specs=[vmem] * 5,
        out_specs=(vmem,) * 7,
        scratch_shapes=[pltpu.VMEM((DS, TOK), BF16)],
        compiler_params=pltpu.CompilerParams(vmem_limit_bytes=VMEM_LIMIT),
        cost_estimate=pl.CostEstimate(
            flops=2 * 2 * ROWS * TOK * DS, bytes_accessed=14_000_000, transcendentals=0
        ),
        name="grads",
    )(es, et, coef, ws, wso)


def head_kernel(g_own, g_got, h_own, h_got, out):
    out[...] = (
        dot(g_own[...], h_own[...], ((1,), (1,))) + dot(g_got[...], h_got[...], ((1,), (1,)))
    ).astype(BF16)


def head_call(g_own, g_got, h_own, h_got):
    step = 640
    whole = pl.BlockSpec((ROWS, TOK), lambda i: (0, 0))
    some = pl.BlockSpec((step, TOK), lambda i: (i, 0))
    return pl.pallas_call(
        head_kernel,
        out_shape=jax.ShapeDtypeStruct((ROWS, DS), BF16),
        grid=(DS // step,),
        in_specs=[whole, whole, some, some],
        out_specs=pl.BlockSpec((ROWS, step), lambda i: (0, i)),
        compiler_params=pltpu.CompilerParams(vmem_limit_bytes=VMEM_LIMIT),
        cost_estimate=pl.CostEstimate(
            flops=2 * 2 * ROWS * TOK * DS, bytes_accessed=10_000_000, transcendentals=0
        ),
        name="head",
    )(g_own, g_got, h_own, h_got)


def merge(stats):
    top = stats[0][0:2]
    for s in stats[1:]:
        top = jnp.maximum(top, s[0:2])
    total = jnp.zeros_like(stats[0][2:5])
    for s in stats:
        scale = jnp.exp(s[0:2] - top)
        total = total + s[2:5] * jnp.concatenate([scale, scale[1:2]], axis=0)
    return jnp.concatenate([top, total, stats[0][5:8]], axis=0)


def per_device(student_hidden, teacher_hidden, student_head, teacher_head, row_weight):
    zl, c, x, y, zh = place()

    teacher_other = send(teacher_head, CORE)
    student_other = send(student_head, CORE)

    mine = jnp.concatenate([student_hidden.T, teacher_hidden.T], axis=0)
    pair = send(mine, PAIR)
    both = jnp.concatenate(
        [jnp.where(zl == 0, mine, pair), jnp.where(zl == 0, pair, mine)], axis=1
    )
    around = (both,) + ring(both, ZH)
    ordered = [lax.select_n((zh - q) & 3, *around) for q in range(4)]
    block = jnp.concatenate([o[:80] for o in ordered] + [o[80:] for o in ordered], axis=0)
    line = jnp.stack((block,) + ring(block, FIRST))
    before, after = send(line, SECOND[1]), send(line, SECOND[3])
    far_low, far_high = send(before[:2], SECOND[1]), send(after[2:], SECOND[3])
    parts = (line, before, after, far_low, far_high)

    es, et, local, hidden_own = logits_call(
        parts, student_head, student_other, teacher_head, teacher_other
    )
    hidden_got = send(hidden_own, CORE)

    stats = merge((local, send(local, PAIR)))
    for perms in (ZH, FIRST, SECOND):
        stats = merge((stats,) + ring(stats, perms))
    student_max, teacher_max, student_total, teacher_total, cross = (stats[i] for i in range(5))
    kl_both = (
        cross / teacher_total
        - teacher_max
        - jnp.log(teacher_total)
        + student_max
        + jnp.log(student_total)
    )
    kl_rows = lax.dynamic_slice_in_dim(kl_both, zl * 128, 128, 0)
    weight = lax.dynamic_index_in_dim(row_weight.reshape(2, 2, 128), c, 1, False).reshape(TOK)
    coef = jnp.stack(
        [
            weight * (jnp.exp(local[0] - student_max) / student_total),
            weight * (jnp.exp(local[1] - teacher_max) / teacher_total),
        ]
    )
    coef = jnp.concatenate([coef, jnp.zeros((6, TOK), F32)], axis=0)

    g_own, g_oth, o0, o1, o3, o2a, o2b = grads_call(es, et, coef, student_head, student_other)
    low, high = send(o2a, SECOND[1]), send(o2b, SECOND[3])
    g_got = send(g_oth, CORE)
    r1 = send(jnp.concatenate([(o1[:2].astype(F32) + low.astype(F32)).astype(BF16), o1[2:]]), SECOND[1])
    r3 = send(jnp.concatenate([o3[:2], (o3[2:].astype(F32) + high.astype(F32)).astype(BF16)]), SECOND[3])
    head_grad = head_call(g_own, g_got, hidden_own, hidden_got)
    r1, r3, head_grad = lax.optimization_barrier((r1, r3, head_grad))

    sums = o0.astype(F32) + (r1.astype(F32) + r3.astype(F32))
    r1, r3, r2 = (send(sums[k].astype(BF16), FIRST[k]) for k in (1, 3, 2))
    sums = (sums[0] + (r1.astype(F32) + r3.astype(F32)) + r2.astype(F32)).reshape(4, 80, TOK)
    narrow = sums.astype(BF16)
    r1, r3, r2 = (
        send(lax.dynamic_index_in_dim(narrow, (zh + k) & 3, 0, False), ZH[k]) for k in (1, 3, 2)
    )
    sums = lax.dynamic_index_in_dim(sums, zh, 0, False) + (r1.astype(F32) + r3.astype(F32)) + r2.astype(F32)
    low, high = sums[:, :128], sums[:, 128:]
    got = send(jnp.where(zl == 0, high, low), PAIR)
    hidden_grad = (jnp.where(zl == 0, low, high) + got).T
    return (kl_rows, hidden_grad, head_grad)


def solution(mesh):
    placed = (
        P("pipe", "vocab"),
        P("pipe", "vocab"),
        P(("pipe", "vocab"), None),
        P(("pipe", "vocab"), None),
        P(),
    )
    return jax.shard_map(
        per_device,
        mesh=mesh,
        in_specs=placed,
        out_specs=(P("pipe"), P("pipe", "vocab"), P(("pipe", "vocab"), None)),
        check_vma=False,
    )
```

```python
import jax
import jax.numpy as jnp
from jax import lax
from jax.experimental import pallas as pl
from jax.experimental.pallas import tpu as pltpu
from jax.sharding import PartitionSpec as P

DS, DT = 5120, 4096
ROWS = 384
TOK = 256
NS, NT = 320, 256
AXES = ("pipe", "vocab")
F32, BF16 = jnp.float32, jnp.bfloat16
VMEM_LIMIT = 24 * 1024 * 1024


def coords(i):
    p, v = divmod(i, 64)
    return p >> 1, p & 1, v >> 4, (v >> 2) & 3, v & 3


def index(zl, c, x, y, zh):
    return (zl * 2 + c) * 64 + x * 16 + y * 4 + zh


def perm(move):
    return [(i, index(*move(*coords(i)))) for i in range(256)]


PAIR = perm(lambda zl, c, x, y, zh: (1 - zl, c, x, y, zh))
CORE = perm(lambda zl, c, x, y, zh: (zl, 1 - c, x, y, zh))
ZH = {k: perm(lambda zl, c, x, y, zh, k=k: (zl, c, x, y, (zh + k) % 4)) for k in (1, 2, 3)}
FIRST = {
    k: perm(lambda zl, c, x, y, zh, k=k: (zl, c, (x + k * (1 - c)) % 4, (y + k * c) % 4, zh))
    for k in (1, 2, 3)
}
SECOND = {
    k: perm(lambda zl, c, x, y, zh, k=k: (zl, c, (x + k * c) % 4, (y + k * (1 - c)) % 4, zh))
    for k in (1, 2, 3)
}


def send(value, pairs):
    return lax.ppermute(value, AXES, pairs)


def ring(value, perms):
    got = {k: send(value, perms[k]) for k in (1, 3, 2)}
    return got[1], got[2], got[3]


def place():
    p, v = lax.axis_index("pipe"), lax.axis_index("vocab")
    return p >> 1, p & 1, v >> 4, (v >> 2) & 3, v & 3


def block_at(c, x, y, first, second):
    in_x = jnp.where(c == 0, first, second)
    in_y = jnp.where(c == 0, second, first)
    return ((x + in_x) & 3) * 4 + ((y + in_y) & 3)


def dot(a, b, dims):
    return lax.dot_general(a, b, (dims, ((), ())), preferred_element_type=F32)


def logits_kernel(
    t0, t1, t3, t2a, t2b, ws, wso, wto, wt, es_out, et_out, st_ref, hs_out, wso_out, hs, ht, es_ref, et_ref, wtb, sem
):
    _, c, x, y, _ = place()
    teacher_in = pltpu.make_async_copy(wt, wtb, sem.at[0])
    keep = pltpu.make_async_copy(wso, wso_out, sem.at[1])
    teacher_in.start()
    keep.start()
    parts = [(0, t0, 0, range(4)), (1, t1, 0, range(4)), (3, t3, 0, range(4))]
    parts += [(2, t2a, 0, range(2)), (2, t2b, 2, range(2, 4))]
    for j, t, base, lines in parts:
        for i in lines:
            at = block_at(c, x, y, (4 - i) & 3, (4 - j) & 3)
            hs[pl.ds(pl.multiple_of(at * NS, NS), NS)] = t[i - base, 0:NS]
            ht[pl.ds(pl.multiple_of(at * NT, NT), NT)] = t[i - base, NS : NS + NT]
    hidden = pltpu.make_async_copy(hs, hs_out, sem.at[2])
    hidden.start()
    es_ref[:ROWS] = dot(ws[...], hs[...], ((1,), (0,)))
    es_ref[ROWS:] = dot(wso[...], hs[...], ((1,), (0,)))
    et_ref[ROWS:] = dot(wto[...], ht[...], ((1,), (0,)))
    teacher_in.wait()
    et_ref[:ROWS] = dot(wtb[...], ht[...], ((1,), (0,)))
    s, t = es_ref[...], et_ref[...]
    sm = jnp.max(s, axis=0, keepdims=True)
    tm = jnp.max(t, axis=0, keepdims=True)
    es, et = jnp.exp(s - sm), jnp.exp(t - tm)
    st_ref[0:1] = sm
    st_ref[1:2] = tm
    st_ref[2:3] = jnp.sum(es, axis=0, keepdims=True)
    st_ref[3:4] = jnp.sum(et, axis=0, keepdims=True)
    st_ref[4:5] = jnp.sum(et * (t - s), axis=0, keepdims=True)
    st_ref[5:8] = jnp.zeros((3, TOK), F32)
    es_ref[...] = es
    et_ref[...] = et
    student_out = pltpu.make_async_copy(es_ref, es_out, sem.at[3])
    teacher_out = pltpu.make_async_copy(et_ref, et_out, sem.at[4])
    student_out.start()
    teacher_out.start()
    for copy in (keep, hidden, student_out, teacher_out):
        copy.wait()


def logits_call(parts, ws, wso, wt, wto):
    vmem = pl.BlockSpec(memory_space=pltpu.VMEM)
    hbm = pl.BlockSpec(memory_space=pltpu.HBM)
    return pl.pallas_call(
        logits_kernel,
        out_shape=(
            jax.ShapeDtypeStruct((2 * ROWS, TOK), F32),
            jax.ShapeDtypeStruct((2 * ROWS, TOK), F32),
            jax.ShapeDtypeStruct((8, TOK), F32),
            jax.ShapeDtypeStruct((DS, TOK), BF16),
            jax.ShapeDtypeStruct((ROWS, DS), BF16),
        ),
        in_specs=[vmem] * 8 + [hbm],
        out_specs=(hbm, hbm, vmem, hbm, hbm),
        scratch_shapes=[
            pltpu.VMEM((DS, TOK), BF16),
            pltpu.VMEM((DT, TOK), BF16),
            pltpu.VMEM((2 * ROWS, TOK), F32),
            pltpu.VMEM((2 * ROWS, TOK), F32),
            pltpu.VMEM((ROWS, DT), BF16),
            pltpu.SemaphoreType.DMA((5,)),
        ],
        compiler_params=pltpu.CompilerParams(vmem_limit_bytes=VMEM_LIMIT),
        cost_estimate=pl.CostEstimate(
            flops=2 * 2 * ROWS * TOK * (DS + DT), bytes_accessed=22_000_000, transcendentals=4 * ROWS * TOK
        ),
        name="logits",
    )(*parts, ws, wso, wto, wt)


def merged(stats):
    top = stats[0][0:2]
    for s in stats[1:]:
        top = jnp.maximum(top, s[0:2])
    totals, cross = jnp.zeros_like(top), jnp.zeros_like(top[0:1])
    for s in stats:
        scale = jnp.exp(s[0:2] - top)
        totals = totals + s[2:4] * scale
        cross = cross + s[4:5] * scale[1:2]
    return top, totals, cross


def merge_kernel(*refs):
    top, totals, cross = merged([r[...] for r in refs[:-1]])
    refs[-1][0:2] = top
    refs[-1][2:4] = totals
    refs[-1][4:5] = cross
    refs[-1][5:8] = jnp.zeros((3, TOK), F32)


def merge(stats):
    vmem = pl.BlockSpec(memory_space=pltpu.VMEM)
    return pl.pallas_call(
        merge_kernel,
        out_shape=jax.ShapeDtypeStruct((8, TOK), F32),
        in_specs=[vmem] * len(stats),
        out_specs=vmem,
        name="merge",
    )(*stats)


CHUNK = 1280


def grads_kernel(
    s0, s1, s2, s3, local, weight, es_in, et_in, ws, wso,
    st_out, g_own, g_oth, o0, o1, o3, o2a, o2b, es, et, wsb, acc, esem, wsem,
):
    _, c, x, y, _ = place()
    terms = [
        pltpu.make_async_copy(es_in, es, esem.at[0]),
        pltpu.make_async_copy(et_in, et, esem.at[1]),
    ]
    weights = []
    for n in range(DS // CHUNK):
        cols = pl.ds(n * CHUNK, CHUNK)
        for half, src in enumerate((ws, wso)):
            weights.append(
                pltpu.make_async_copy(
                    src.at[:, cols], wsb.at[pl.ds(half * ROWS, ROWS), cols], wsem.at[2 * n + half]
                )
            )
    for copy in terms + weights:
        copy.start()
    top, totals, cross = merged([s0[...], s1[...], s2[...], s3[...]])
    st_out[0:2] = top
    st_out[2:4] = totals
    st_out[4:5] = cross
    st_out[5:8] = jnp.zeros((3, TOK), F32)
    coef = weight[0:1] * (jnp.exp(local[0:2] - top) / totals)
    for copy in terms:
        copy.wait()
    g = (es[...] * coef[0:1] - et[...] * coef[1:2]).astype(BF16)
    g_own[...] = g[:ROWS]
    g_oth[...] = g[ROWS:]
    for n in range(DS // CHUNK):
        weights[2 * n].wait()
        weights[2 * n + 1].wait()
        cols = slice(n * CHUNK, (n + 1) * CHUNK)
        acc[cols] = dot(g, wsb[:, cols], ((0,), (0,))).astype(BF16).T
    outs = [(0, o0, 0, range(4)), (1, o1, 0, range(4)), (3, o3, 0, range(4))]
    outs += [(2, o2a, 0, range(2)), (2, o2b, 2, range(2, 4))]
    for k, o, base, lines in outs:
        for r in lines:
            at = block_at(c, x, y, r, k)
            o[r - base] = acc[pl.ds(pl.multiple_of(at * NS, NS), NS)]


def grads_call(stats, local, weight, es, et, ws, wso):
    vmem = pl.BlockSpec(memory_space=pltpu.VMEM)
    hbm = pl.BlockSpec(memory_space=pltpu.HBM)
    whole = jax.ShapeDtypeStruct((4, NS, TOK), BF16)
    half = jax.ShapeDtypeStruct((2, NS, TOK), BF16)
    rows = jax.ShapeDtypeStruct((ROWS, TOK), BF16)
    return pl.pallas_call(
        grads_kernel,
        out_shape=(
            jax.ShapeDtypeStruct((8, TOK), F32), rows, rows, whole, whole, whole, half, half,
        ),
        in_specs=[vmem] * 6 + [hbm] * 4,
        out_specs=(vmem,) * 8,
        scratch_shapes=[
            pltpu.VMEM((2 * ROWS, TOK), F32),
            pltpu.VMEM((2 * ROWS, TOK), F32),
            pltpu.VMEM((2 * ROWS, DS), BF16),
            pltpu.VMEM((DS, TOK), BF16),
            pltpu.SemaphoreType.DMA((2,)),
            pltpu.SemaphoreType.DMA((8,)),
        ],
        compiler_params=pltpu.CompilerParams(vmem_limit_bytes=VMEM_LIMIT),
        cost_estimate=pl.CostEstimate(
            flops=2 * 2 * ROWS * TOK * DS, bytes_accessed=14_000_000, transcendentals=0
        ),
        name="grads",
    )(*stats, local, weight, es, et, ws, wso)


def head_kernel(g_own, g_got, h_own, h_got, out):
    out[...] = (
        dot(g_own[...], h_own[...], ((1,), (1,))) + dot(g_got[...], h_got[...], ((1,), (1,)))
    ).astype(BF16)


def head_call(g_own, g_got, h_own, h_got):
    step = 640
    whole = pl.BlockSpec((ROWS, TOK), lambda i: (0, 0))
    some = pl.BlockSpec((step, TOK), lambda i: (i, 0))
    return pl.pallas_call(
        head_kernel,
        out_shape=jax.ShapeDtypeStruct((ROWS, DS), BF16),
        grid=(DS // step,),
        in_specs=[whole, whole, some, some],
        out_specs=pl.BlockSpec((ROWS, step), lambda i: (0, i)),
        compiler_params=pltpu.CompilerParams(vmem_limit_bytes=VMEM_LIMIT),
        cost_estimate=pl.CostEstimate(
            flops=2 * 2 * ROWS * TOK * DS, bytes_accessed=10_000_000, transcendentals=0
        ),
        name="head",
    )(g_own, g_got, h_own, h_got)


def per_device(student_hidden, teacher_hidden, student_head, teacher_head, row_weight):
    zl, c, x, y, zh = place()

    teacher_other = send(teacher_head, CORE)
    student_other = send(student_head, CORE)

    mine = jnp.concatenate([student_hidden.T, teacher_hidden.T], axis=0)
    pair = send(mine, PAIR)
    both = jnp.concatenate(
        [jnp.where(zl == 0, mine, pair), jnp.where(zl == 0, pair, mine)], axis=1
    )
    around = (both,) + ring(both, ZH)
    ordered = [lax.select_n((zh - q) & 3, *around) for q in range(4)]
    block = jnp.concatenate([o[:80] for o in ordered] + [o[80:] for o in ordered], axis=0)
    line = jnp.stack((block,) + ring(block, FIRST))
    before, after = send(line, SECOND[1]), send(line, SECOND[3])
    far_low, far_high = send(before[:2], SECOND[1]), send(after[2:], SECOND[3])
    parts = (line, before, after, far_low, far_high)

    es, et, local, hidden_own, student_other = logits_call(
        parts, student_head, student_other, teacher_head, teacher_other
    )
    hidden_got = send(hidden_own, CORE)

    stats = merge((local, send(local, PAIR)))
    for perms in (ZH, FIRST):
        stats = merge((stats,) + ring(stats, perms))
    weight = lax.dynamic_index_in_dim(row_weight.reshape(2, 2, 128), c, 1, False).reshape(1, TOK)
    weight = jnp.broadcast_to(weight, (8, TOK))

    stats, g_own, g_oth, o0, o1, o3, o2a, o2b = grads_call(
        (stats,) + ring(stats, SECOND), local, weight, es, et, student_head, student_other
    )
    student_max, teacher_max, student_total, teacher_total, cross = (stats[i] for i in range(5))
    kl_both = (
        cross / teacher_total
        - teacher_max
        - jnp.log(teacher_total)
        + student_max
        + jnp.log(student_total)
    )
    kl_rows = lax.dynamic_slice_in_dim(kl_both, zl * 128, 128, 0)
    low, high = send(o2a, SECOND[1]), send(o2b, SECOND[3])
    g_got = send(g_oth, CORE)
    r1 = send(jnp.concatenate([(o1[:2].astype(F32) + low.astype(F32)).astype(BF16), o1[2:]]), SECOND[1])
    r3 = send(jnp.concatenate([o3[:2], (o3[2:].astype(F32) + high.astype(F32)).astype(BF16)]), SECOND[3])
    head_grad = head_call(g_own, g_got, hidden_own, hidden_got)
    r1, r3, head_grad = lax.optimization_barrier((r1, r3, head_grad))

    sums = o0.astype(F32) + (r1.astype(F32) + r3.astype(F32))
    r1, r3, r2 = (send(sums[k].astype(BF16), FIRST[k]) for k in (1, 3, 2))
    sums = (sums[0] + (r1.astype(F32) + r3.astype(F32)) + r2.astype(F32)).reshape(4, 80, TOK)
    narrow = sums.astype(BF16)
    r1, r3, r2 = (
        send(lax.dynamic_index_in_dim(narrow, (zh + k) & 3, 0, False), ZH[k]) for k in (1, 3, 2)
    )
    sums = lax.dynamic_index_in_dim(sums, zh, 0, False) + (r1.astype(F32) + r3.astype(F32)) + r2.astype(F32)
    low, high = sums[:, :128], sums[:, 128:]
    got = send(jnp.where(zl == 0, high, low), PAIR)
    hidden_grad = (jnp.where(zl == 0, low, high) + got).T
    return (kl_rows, hidden_grad, head_grad)


def solution(mesh):
    placed = (
        P("pipe", "vocab"),
        P("pipe", "vocab"),
        P(("pipe", "vocab"), None),
        P(("pipe", "vocab"), None),
        P(),
    )
    return jax.shard_map(
        per_device,
        mesh=mesh,
        in_specs=placed,
        out_specs=(P("pipe"), P("pipe", "vocab"), P(("pipe", "vocab"), None)),
        check_vma=False,
    )
```

```python
import jax
import jax.numpy as jnp
from jax import lax
from jax.experimental import pallas as pl
from jax.experimental.pallas import tpu as pltpu
from jax.sharding import PartitionSpec as P

DS, DT = 5120, 4096
ROWS = 384
TOK = 256
NS, NT = 320, 256
AXES = ("zl", "c", "x", "y", "zh")
F32, BF16 = jnp.float32, jnp.bfloat16
VMEM_LIMIT = 20 * 1024 * 1024


def coords(i):
    p, v = divmod(i, 64)
    return p >> 1, p & 1, v >> 4, (v >> 2) & 3, v & 3


def index(zl, c, x, y, zh):
    return (zl * 2 + c) * 64 + x * 16 + y * 4 + zh


def perm(move):
    return [(i, index(*move(*coords(i)))) for i in range(256)]


PAIR = perm(lambda zl, c, x, y, zh: (1 - zl, c, x, y, zh))
CORE = perm(lambda zl, c, x, y, zh: (zl, 1 - c, x, y, zh))
ZH = {k: perm(lambda zl, c, x, y, zh, k=k: (zl, c, x, y, (zh + k) % 4)) for k in (1, 2, 3)}
FIRST = {
    k: perm(lambda zl, c, x, y, zh, k=k: (zl, c, (x + k * (1 - c)) % 4, (y + k * c) % 4, zh))
    for k in (1, 2, 3)
}
SECOND = {
    k: perm(lambda zl, c, x, y, zh, k=k: (zl, c, (x + k * c) % 4, (y + k * (1 - c)) % 4, zh))
    for k in (1, 2, 3)
}


def send(value, pairs):
    return lax.ppermute(value, AXES, pairs)


def ring(value, perms):
    got = {k: send(value, perms[k]) for k in (1, 3, 2)}
    return got[1], got[2], got[3]


def place():
    return tuple(lax.axis_index(a) for a in AXES)


def block_at(c, x, y, first, second):
    in_x = jnp.where(c == 0, first, second)
    in_y = jnp.where(c == 0, second, first)
    return ((x + in_x) & 3) * 4 + ((y + in_y) & 3)


def dot(a, b, dims):
    return lax.dot_general(a, b, (dims, ((), ())), preferred_element_type=F32)


def logits_kernel(t0, t1, t3, t2a, t2b, ws, wso, wt, wto, es_ref, et_ref, st_ref, hs, ht):
    _, c, x, y, _ = place()
    parts = [(0, t0, 0, range(4)), (1, t1, 0, range(4)), (3, t3, 0, range(4))]
    parts += [(2, t2a, 0, range(2)), (2, t2b, 2, range(2, 4))]
    for j, t, base, lines in parts:
        for i in lines:
            at = block_at(c, x, y, (4 - i) & 3, (4 - j) & 3)
            ht[pl.ds(pl.multiple_of(at * NT, NT), NT)] = t[i - base, NS : NS + NT]
            hs[pl.ds(pl.multiple_of(at * NS, NS), NS)] = t[i - base, 0:NS]
    et_ref[:ROWS] = dot(wt[...], ht[...], ((1,), (0,)))
    et_ref[ROWS:] = dot(wto[...], ht[...], ((1,), (0,)))
    es_ref[:ROWS] = dot(ws[...], hs[...], ((1,), (0,)))
    es_ref[ROWS:] = dot(wso[...], hs[...], ((1,), (0,)))
    s, t = es_ref[...], et_ref[...]
    sm = jnp.max(s, axis=0, keepdims=True)
    tm = jnp.max(t, axis=0, keepdims=True)
    es, et = jnp.exp(s - sm), jnp.exp(t - tm)
    st_ref[0:1] = sm
    st_ref[1:2] = tm
    st_ref[2:3] = jnp.sum(es, axis=0, keepdims=True)
    st_ref[3:4] = jnp.sum(et, axis=0, keepdims=True)
    st_ref[4:5] = jnp.sum(et * (t - s), axis=0, keepdims=True)
    st_ref[5:8] = jnp.zeros((3, TOK), F32)
    es_ref[...] = es
    et_ref[...] = et


def logits_call(parts, ws, wso, wt, wto):
    vmem = pl.BlockSpec(memory_space=pltpu.VMEM)
    return pl.pallas_call(
        logits_kernel,
        out_shape=(
            jax.ShapeDtypeStruct((2 * ROWS, TOK), F32),
            jax.ShapeDtypeStruct((2 * ROWS, TOK), F32),
            jax.ShapeDtypeStruct((8, TOK), F32),
            jax.ShapeDtypeStruct((DS, TOK), BF16),
        ),
        in_specs=[vmem] * 9,
        out_specs=(vmem,) * 4,
        scratch_shapes=[pltpu.VMEM((DT, TOK), BF16)],
        compiler_params=pltpu.CompilerParams(vmem_limit_bytes=VMEM_LIMIT),
        cost_estimate=pl.CostEstimate(
            flops=2 * 2 * ROWS * TOK * (DS + DT), bytes_accessed=22_000_000, transcendentals=4 * ROWS * TOK
        ),
        name="logits",
    )(*parts, ws, wso, wt, wto)


CHUNK = 1280


def grads_kernel(
    stats, local, weights, es_ref, et_ref, ws, wso, kl_ref, g_own, g_oth, o0, o1, o3, o2a, o2b, acc
):
    zl, c, x, y, _ = place()
    top, totals = stats[0:2], stats[2:4]
    kl = stats[4:5] / totals[1:2] - top[1:2] - jnp.log(totals[1:2]) + top[0:1] + jnp.log(totals[0:1])
    kl_ref[...] = jnp.where(zl == 0, kl[:, :128], kl[:, 128:])
    weight = jnp.concatenate(
        [jnp.where(c == 0, weights[i : i + 1], weights[i + 1 : i + 2]) for i in (0, 2)], axis=1
    )
    coef = weight * (jnp.exp(local[0:2] - top) / totals)
    g = (es_ref[...] * coef[0:1] - et_ref[...] * coef[1:2]).astype(BF16)
    g_own[...] = g[:ROWS]
    g_oth[...] = g[ROWS:]
    for n in range(DS // CHUNK):
        cols = slice(n * CHUNK, (n + 1) * CHUNK)
        part = dot(g[:ROWS], ws[:, cols], ((0,), (0,))) + dot(g[ROWS:], wso[:, cols], ((0,), (0,)))
        acc[cols] = part.astype(BF16).T
    outs = [(0, o0, 0, range(4)), (1, o1, 0, range(4)), (3, o3, 0, range(4))]
    outs += [(2, o2a, 0, range(2)), (2, o2b, 2, range(2, 4))]
    for k, o, base, lines in outs:
        for r in lines:
            at = block_at(c, x, y, r, k)
            o[r - base] = acc[pl.ds(pl.multiple_of(at * NS, NS), NS)]


def grads_call(stats, local, weights, es, et, ws, wso):
    vmem = pl.BlockSpec(memory_space=pltpu.VMEM)
    whole = jax.ShapeDtypeStruct((4, NS, TOK), BF16)
    half = jax.ShapeDtypeStruct((2, NS, TOK), BF16)
    rows = jax.ShapeDtypeStruct((ROWS, TOK), BF16)
    return pl.pallas_call(
        grads_kernel,
        out_shape=(jax.ShapeDtypeStruct((1, 128), F32), rows, rows, whole, whole, whole, half, half),
        in_specs=[vmem] * 7,
        out_specs=(vmem,) * 8,
        scratch_shapes=[pltpu.VMEM((DS, TOK), BF16)],
        compiler_params=pltpu.CompilerParams(vmem_limit_bytes=VMEM_LIMIT),
        cost_estimate=pl.CostEstimate(
            flops=2 * 2 * ROWS * TOK * DS, bytes_accessed=14_000_000, transcendentals=0
        ),
        name="grads",
    )(stats, local, weights, es, et, ws, wso)


def head_kernel(g_own, g_got, h_own, h_got, out):
    out[...] = (
        dot(g_own[...], h_own[...], ((1,), (1,))) + dot(g_got[...], h_got[...], ((1,), (1,)))
    ).astype(BF16)


def head_call(g_own, g_got, h_own, h_got):
    step = 640
    whole = pl.BlockSpec((ROWS, TOK), lambda i: (0, 0))
    some = pl.BlockSpec((step, TOK), lambda i: (i, 0))
    return pl.pallas_call(
        head_kernel,
        out_shape=jax.ShapeDtypeStruct((ROWS, DS), BF16),
        grid=(DS // step,),
        in_specs=[whole, whole, some, some],
        out_specs=pl.BlockSpec((ROWS, step), lambda i: (0, i)),
        compiler_params=pltpu.CompilerParams(vmem_limit_bytes=VMEM_LIMIT),
        cost_estimate=pl.CostEstimate(
            flops=2 * 2 * ROWS * TOK * DS, bytes_accessed=10_000_000, transcendentals=0
        ),
        name="head",
    )(g_own, g_got, h_own, h_got)


def merge(stats):
    top = stats[0][0:2]
    for s in stats[1:]:
        top = jnp.maximum(top, s[0:2])
    total = jnp.zeros_like(stats[0][2:5])
    for s in stats:
        scale = jnp.exp(s[0:2] - top)
        total = total + s[2:5] * jnp.concatenate([scale, scale[1:2]], axis=0)
    return jnp.concatenate([top, total, stats[0][5:8]], axis=0)


def per_device(student_hidden, teacher_hidden, student_head, teacher_head, row_weight):
    teacher_other = send(teacher_head, CORE)
    student_other = send(student_head, CORE)

    mine = jnp.concatenate([student_hidden.T, teacher_hidden.T], axis=0)
    along = lax.all_to_all(jnp.broadcast_to(mine, (8, 144, 128)), ("zl", "zh"), 0, 0)
    along = jnp.concatenate([along[:4], along[4:]], axis=2)
    block = jnp.concatenate([along[:, :80].reshape(NS, TOK), along[:, 80:].reshape(NT, TOK)], axis=0)
    line = jnp.stack((block,) + ring(block, FIRST))
    before, after = send(line, SECOND[1]), send(line, SECOND[3])
    far_low, far_high = send(before[:2], SECOND[1]), send(after[2:], SECOND[3])
    parts = (line, before, after, far_low, far_high)

    es, et, local, hidden_own = logits_call(
        parts, student_head, student_other, teacher_head, teacher_other
    )
    hidden_got = send(hidden_own, CORE)

    stats = merge((local, send(local, PAIR)))
    for perms in (ZH, FIRST, SECOND):
        stats = merge((stats,) + ring(stats, perms))
    kl_rows, g_own, g_oth, o0, o1, o3, o2a, o2b = grads_call(
        stats, local, row_weight.reshape(4, 128), es, et, student_head, student_other
    )
    low, high = send(o2a, SECOND[1]), send(o2b, SECOND[3])
    g_got = send(g_oth, CORE)
    r1 = send(jnp.concatenate([(o1[:2].astype(F32) + low.astype(F32)).astype(BF16), o1[2:]]), SECOND[1])
    r3 = send(jnp.concatenate([o3[:2], (o3[2:].astype(F32) + high.astype(F32)).astype(BF16)]), SECOND[3])
    head_grad = head_call(g_own, g_got, hidden_own, hidden_got)
    r1, r3, head_grad = lax.optimization_barrier((r1, r3, head_grad))

    sums = o0.astype(F32) + (r1.astype(F32) + r3.astype(F32))
    r1, r3, r2 = (send(sums[k].astype(BF16), FIRST[k]) for k in (1, 3, 2))
    sums = sums[0] + (r1.astype(F32) + r3.astype(F32)) + r2.astype(F32)
    sums = jnp.concatenate([sums[:, :128], sums[:, 128:]], axis=0).reshape(8, 80, 128)
    hidden_grad = jnp.sum(lax.all_to_all(sums, ("zl", "zh"), 0, 0), axis=0).T
    return (kl_rows.reshape(128), hidden_grad, head_grad)


def solution(mesh):
    fine = jax.sharding.Mesh(mesh.devices.reshape(2, 2, 4, 4, 4), AXES)
    pipe, vocab = AXES[:2], AXES[2:]
    placed = (P(pipe, vocab), P(pipe, vocab), P(AXES, None), P(AXES, None), P())
    return jax.shard_map(
        per_device,
        mesh=fine,
        in_specs=placed,
        out_specs=(P(pipe), P(pipe, vocab), P(AXES, None)),
        check_vma=False,
    )
```

```python
import jax
import jax.numpy as jnp
from jax import lax
from jax.experimental import pallas as pl
from jax.experimental.pallas import tpu as pltpu
from jax.sharding import PartitionSpec as P

DS, DT = 5120, 4096
ROWS = 384
TOK = 256
NS, NT = 320, 256
WIDE = 384
AXES = ("zl", "c", "x", "y", "zh")
F32, BF16 = jnp.float32, jnp.bfloat16
VMEM_LIMIT = 20 * 1024 * 1024


def coords(i):
    p, v = divmod(i, 64)
    return p >> 1, p & 1, v >> 4, (v >> 2) & 3, v & 3


def index(zl, c, x, y, zh):
    return (zl * 2 + c) * 64 + x * 16 + y * 4 + zh


def perm(move):
    return [(i, index(*move(*coords(i)))) for i in range(256)]


PAIR = perm(lambda zl, c, x, y, zh: (1 - zl, c, x, y, zh))
CORE = perm(lambda zl, c, x, y, zh: (zl, 1 - c, x, y, zh))
ZH = {k: perm(lambda zl, c, x, y, zh, k=k: (zl, c, x, y, (zh + k) % 4)) for k in (1, 2, 3)}
FIRST = {
    k: perm(lambda zl, c, x, y, zh, k=k: (zl, c, (x + k * (1 - c)) % 4, (y + k * c) % 4, zh))
    for k in (1, 2, 3)
}
SECOND = {
    k: perm(lambda zl, c, x, y, zh, k=k: (zl, c, (x + k * c) % 4, (y + k * (1 - c)) % 4, zh))
    for k in (1, 2, 3)
}


def send(value, pairs):
    return lax.ppermute(value, AXES, pairs)


def ring(value, perms):
    got = {k: send(value, perms[k]) for k in (1, 3, 2)}
    return got[1], got[2], got[3]


def place():
    return tuple(lax.axis_index(a) for a in AXES)


def block_at(c, x, y, first, second):
    in_x = jnp.where(c == 0, first, second)
    in_y = jnp.where(c == 0, second, first)
    return ((x + in_x) & 3) * 4 + ((y + in_y) & 3)


def dot(a, b, dims):
    return lax.dot_general(a, b, (dims, ((), ())), preferred_element_type=F32)


def window(at):
    start = pl.multiple_of(((at * 5) >> 1) * 128, 128)
    return pl.ds(start, WIDE), pl.multiple_of((at & 1) * 64, 64)


def near_kernel(t0, t1, t3, ws, wso, wt, wto, s_ref, t_ref, hs, ht):
    _, c, x, y, _ = place()
    for j, t in ((0, t0), (1, t1), (3, t3), (2, None)):
        for i in range(4):
            at = block_at(c, x, y, (4 - i) & 3, (4 - j) & 3)
            rows_s = pl.ds(pl.multiple_of(at * NS, NS), NS)
            rows_t = pl.ds(pl.multiple_of(at * NT, NT), NT)
            if t is None:
                hs[rows_s] = jnp.zeros((NS, TOK), BF16)
                ht[rows_t] = jnp.zeros((NT, TOK), BF16)
            else:
                hs[rows_s] = t[i, 0:NS]
                ht[rows_t] = t[i, NS : NS + NT]
    t_ref[:ROWS] = dot(wt[...], ht[...], ((1,), (0,)))
    t_ref[ROWS:] = dot(wto[...], ht[...], ((1,), (0,)))
    s_ref[:ROWS] = dot(ws[...], hs[...], ((1,), (0,)))
    s_ref[ROWS:] = dot(wso[...], hs[...], ((1,), (0,)))


def far_kernel(
    t2a, t2b, s_in, t_in, hs_in, ws, wso, wt, wto, es_ref, et_ref, st_ref, hs, pads
):
    _, c, x, y, _ = place()
    s_ref, t_ref = es_ref, et_ref
    hs[...] = hs_in[...]
    s_ref[...] = s_in[...]
    t_ref[...] = t_in[...]
    for i in range(4):
        line = t2a[i] if i < 2 else t2b[i - 2]
        at = block_at(c, x, y, (4 - i) & 3, 2)
        hs[pl.ds(pl.multiple_of(at * NS, NS), NS)] = line[0:NS]
        cols, first = window(at)
        pads[i] = jnp.zeros((WIDE, TOK), BF16)
        pads[i, pl.ds(first, NS)] = line[0:NS]
        cols_t = pl.ds(pl.multiple_of(at * NT, NT), NT)
        s_ref[:ROWS] += dot(ws[:, cols], pads[i], ((1,), (0,)))
        s_ref[ROWS:] += dot(wso[:, cols], pads[i], ((1,), (0,)))
        t_ref[:ROWS] += dot(wt[:, cols_t], line[NS:], ((1,), (0,)))
        t_ref[ROWS:] += dot(wto[:, cols_t], line[NS:], ((1,), (0,)))
    s, t = s_ref[...], t_ref[...]
    sm = jnp.max(s, axis=0, keepdims=True)
    tm = jnp.max(t, axis=0, keepdims=True)
    es, et = jnp.exp(s - sm), jnp.exp(t - tm)
    st_ref[0:1] = sm
    st_ref[1:2] = tm
    st_ref[2:3] = jnp.sum(es, axis=0, keepdims=True)
    st_ref[3:4] = jnp.sum(et, axis=0, keepdims=True)
    st_ref[4:5] = jnp.sum(et * (t - s), axis=0, keepdims=True)
    st_ref[5:8] = jnp.zeros((3, TOK), F32)
    es_ref[...] = es
    et_ref[...] = et


def vmem_call(kernel, name, outs, scratch, flops, *args):
    vmem = pl.BlockSpec(memory_space=pltpu.VMEM)
    return pl.pallas_call(
        kernel,
        out_shape=tuple(jax.ShapeDtypeStruct(*o) for o in outs),
        in_specs=[vmem] * len(args),
        out_specs=(vmem,) * len(outs),
        scratch_shapes=[pltpu.VMEM(*o) for o in scratch],
        compiler_params=pltpu.CompilerParams(vmem_limit_bytes=VMEM_LIMIT),
        cost_estimate=pl.CostEstimate(flops=flops, bytes_accessed=14_000_000, transcendentals=0),
        name=name,
    )(*args)


LOGITS = ((2 * ROWS, TOK), F32)
HIDDEN = ((DS, TOK), BF16)


def near_call(t0, t1, t3, *weights):
    flops = 2 * 2 * ROWS * TOK * (DS + DT)
    outs = (LOGITS, LOGITS, HIDDEN)
    return vmem_call(near_kernel, "near", outs, [((DT, TOK), BF16)], flops, t0, t1, t3, *weights)


def far_call(*args):
    flops = 2 * 2 * ROWS * TOK * (DS + DT) // 3
    outs = (LOGITS, LOGITS, ((8, TOK), F32), HIDDEN)
    return vmem_call(far_kernel, "far", outs, [((4, WIDE, TOK), BF16)], flops, *args)


CHUNK = 1280


def opposite_kernel(
    stats, local, weights, es_ref, et_ref, ws, wso, kl_ref, g_own, g_oth, o2a, o2b, part
):
    zl, c, x, y, _ = place()
    top, totals = stats[0:2], stats[2:4]
    kl = stats[4:5] / totals[1:2] - top[1:2] - jnp.log(totals[1:2]) + top[0:1] + jnp.log(totals[0:1])
    kl_ref[...] = jnp.where(zl == 0, kl[:, :128], kl[:, 128:])
    weight = jnp.concatenate(
        [jnp.where(c == 0, weights[i : i + 1], weights[i + 1 : i + 2]) for i in (0, 2)], axis=1
    )
    coef = weight * (jnp.exp(local[0:2] - top) / totals)
    g = (es_ref[...] * coef[0:1] - et_ref[...] * coef[1:2]).astype(BF16)
    g_own[...] = g[:ROWS]
    g_oth[...] = g[ROWS:]
    for r in range(4):
        cols, first = window(block_at(c, x, y, r, 2))
        whole = dot(g[:ROWS], ws[:, cols], ((0,), (0,))) + dot(g[ROWS:], wso[:, cols], ((0,), (0,)))
        part[r] = whole.astype(BF16).T
        if r < 2:
            o2a[r] = part[r, pl.ds(first, NS)]
        else:
            o2b[r - 2] = part[r, pl.ds(first, NS)]


def rest_kernel(g_own, g_oth, ws, wso, o0, o1, o3, acc):
    _, c, x, y, _ = place()
    for n in range(DS // CHUNK):
        cols = slice(n * CHUNK, (n + 1) * CHUNK)
        part = dot(g_own[...], ws[:, cols], ((0,), (0,))) + dot(g_oth[...], wso[:, cols], ((0,), (0,)))
        acc[cols] = part.astype(BF16).T
    for k, o in ((0, o0), (1, o1), (3, o3)):
        for r in range(4):
            at = block_at(c, x, y, r, k)
            o[r] = acc[pl.ds(pl.multiple_of(at * NS, NS), NS)]


def opposite_call(*args):
    rows, half = ((ROWS, TOK), BF16), ((2, NS, TOK), BF16)
    outs = (((1, 128), F32), rows, rows, half, half)
    flops = 2 * 2 * ROWS * TOK * DS // 3
    return vmem_call(opposite_kernel, "opposite", outs, [((4, WIDE, TOK), BF16)], flops, *args)


def rest_call(*args):
    outs = (((4, NS, TOK), BF16),) * 3
    return vmem_call(rest_kernel, "rest", outs, [HIDDEN], 2 * 2 * ROWS * TOK * DS, *args)


def head_kernel(g_own, g_got, h_own, h_got, out):
    out[...] = (
        dot(g_own[...], h_own[...], ((1,), (1,))) + dot(g_got[...], h_got[...], ((1,), (1,)))
    ).astype(BF16)


def head_call(g_own, g_got, h_own, h_got):
    step = 640
    whole = pl.BlockSpec((ROWS, TOK), lambda i: (0, 0))
    some = pl.BlockSpec((step, TOK), lambda i: (i, 0))
    return pl.pallas_call(
        head_kernel,
        out_shape=jax.ShapeDtypeStruct((ROWS, DS), BF16),
        grid=(DS // step,),
        in_specs=[whole, whole, some, some],
        out_specs=pl.BlockSpec((ROWS, step), lambda i: (0, i)),
        compiler_params=pltpu.CompilerParams(vmem_limit_bytes=VMEM_LIMIT),
        cost_estimate=pl.CostEstimate(
            flops=2 * 2 * ROWS * TOK * DS, bytes_accessed=10_000_000, transcendentals=0
        ),
        name="head",
    )(g_own, g_got, h_own, h_got)


def merge(stats):
    top = stats[0][0:2]
    for s in stats[1:]:
        top = jnp.maximum(top, s[0:2])
    total = jnp.zeros_like(stats[0][2:5])
    for s in stats:
        scale = jnp.exp(s[0:2] - top)
        total = total + s[2:5] * jnp.concatenate([scale, scale[1:2]], axis=0)
    return jnp.concatenate([top, total, stats[0][5:8]], axis=0)


def per_device(student_hidden, teacher_hidden, student_head, teacher_head, row_weight):
    teacher_other = send(teacher_head, CORE)
    student_other = send(student_head, CORE)

    mine = jnp.concatenate([jnp.broadcast_to(h.T, (8,) + h.T.shape) for h in (student_hidden, teacher_hidden)], axis=1)
    along = lax.all_to_all(mine, ("zl", "zh"), 0, 0)
    along = jnp.concatenate([along[:4], along[4:]], axis=2)
    block = jnp.concatenate([along[:, :80].reshape(NS, TOK), along[:, 80:].reshape(NT, TOK)], axis=0)
    line = jnp.stack((block,) + ring(block, FIRST))
    before, after = send(line, SECOND[1]), send(line, SECOND[3])
    far_low, far_high = send(before[:2], SECOND[1]), send(after[2:], SECOND[3])

    heads = (student_head, student_other, teacher_head, teacher_other)
    near = near_call(line, before, after, *heads)
    es, et, local, hidden_own = far_call(far_low, far_high, *near, *heads)
    hidden_got = send(hidden_own, CORE)

    stats = merge((local, send(local, PAIR)))
    for perms in (ZH, FIRST, SECOND):
        stats = merge((stats,) + ring(stats, perms))
    kl_rows, g_own, g_oth, o2a, o2b = opposite_call(
        stats, local, row_weight.reshape(4, 128), es, et, student_head, student_other
    )
    low, high = send(o2a, SECOND[1]), send(o2b, SECOND[3])
    g_got = send(g_oth, CORE)
    low, high, g_got, o0, o1, o3 = lax.optimization_barrier(
        (low, high, g_got, *rest_call(g_own, g_oth, student_head, student_other))
    )
    r1 = send(jnp.concatenate([(o1[:2].astype(F32) + low.astype(F32)).astype(BF16), o1[2:]]), SECOND[1])
    r3 = send(jnp.concatenate([o3[:2], (o3[2:].astype(F32) + high.astype(F32)).astype(BF16)]), SECOND[3])
    head_grad = head_call(g_own, g_got, hidden_own, hidden_got)
    r1, r3, head_grad = lax.optimization_barrier((r1, r3, head_grad))

    sums = o0.astype(F32) + (r1.astype(F32) + r3.astype(F32))
    r1, r3, r2 = (send(sums[k].astype(BF16), FIRST[k]) for k in (1, 3, 2))
    sums = sums[0] + (r1.astype(F32) + r3.astype(F32)) + r2.astype(F32)
    sums = jnp.concatenate([sums[:, :128], sums[:, 128:]], axis=0).reshape(8, 80, 128)
    hidden_grad = jnp.sum(lax.all_to_all(sums, ("zl", "zh"), 0, 0), axis=0).T
    return (kl_rows.reshape(128), hidden_grad, head_grad)


def solution(mesh):
    fine = jax.sharding.Mesh(mesh.devices.reshape(2, 2, 4, 4, 4), AXES)
    pipe, vocab = AXES[:2], AXES[2:]
    placed = (P(pipe, vocab), P(pipe, vocab), P(AXES, None), P(AXES, None), P())
    return jax.shard_map(
        per_device,
        mesh=fine,
        in_specs=placed,
        out_specs=(P(pipe), P(pipe, vocab), P(AXES, None)),
        check_vma=False,
    )
```

```python
import jax
import jax.numpy as jnp
from jax import lax
from jax.experimental import pallas as pl
from jax.experimental.pallas import tpu as pltpu
from jax.sharding import PartitionSpec as P

DS, DT = 5120, 4096
ROWS = 384
TOK = 256
NS, NT = 320, 256
WIDE = 384
AXES = ("zl", "c", "x", "y", "zh")
F32, BF16 = jnp.float32, jnp.bfloat16
VMEM_LIMIT = 20 * 1024 * 1024


def coords(i):
    p, v = divmod(i, 64)
    return p >> 1, p & 1, v >> 4, (v >> 2) & 3, v & 3


def index(zl, c, x, y, zh):
    return (zl * 2 + c) * 64 + x * 16 + y * 4 + zh


def perm(move):
    return [(i, index(*move(*coords(i)))) for i in range(256)]


PAIR = perm(lambda zl, c, x, y, zh: (1 - zl, c, x, y, zh))
CORE = perm(lambda zl, c, x, y, zh: (zl, 1 - c, x, y, zh))
ZH = {k: perm(lambda zl, c, x, y, zh, k=k: (zl, c, x, y, (zh + k) % 4)) for k in (1, 2, 3)}
FIRST = {
    k: perm(lambda zl, c, x, y, zh, k=k: (zl, c, (x + k * (1 - c)) % 4, (y + k * c) % 4, zh))
    for k in (1, 2, 3)
}
SECOND = {
    k: perm(lambda zl, c, x, y, zh, k=k: (zl, c, (x + k * c) % 4, (y + k * (1 - c)) % 4, zh))
    for k in (1, 2, 3)
}


def send(value, pairs):
    return lax.ppermute(value, AXES, pairs)


def ring(value, perms):
    got = {k: send(value, perms[k]) for k in (1, 3, 2)}
    return got[1], got[2], got[3]


def place():
    return tuple(lax.axis_index(a) for a in AXES)


def block_at(c, x, y, first, second):
    in_x = jnp.where(c == 0, first, second)
    in_y = jnp.where(c == 0, second, first)
    return ((x + in_x) & 3) * 4 + ((y + in_y) & 3)


def dot(a, b, dims):
    return lax.dot_general(a, b, (dims, ((), ())), preferred_element_type=F32)


def window(at):
    start = pl.multiple_of(((at * 5) >> 1) * 128, 128)
    return pl.ds(start, WIDE), pl.multiple_of((at & 1) * 64, 64)


def spread_kernel(mine, out):
    for i in range(8):
        out[i] = mine[...]


def weave_kernel(along, out):
    for zh in range(4):
        for zl in range(2):
            tokens = slice(zl * 128, (zl + 1) * 128)
            out[zh * 80 : (zh + 1) * 80, tokens] = along[zl * 4 + zh, 0:80]
            out[NS + zh * 64 : NS + (zh + 1) * 64, tokens] = along[zl * 4 + zh, 80:144]


def near_kernel(t0, t1, t3, ws, wso, wt, wto, s_ref, t_ref, hs, ht):
    _, c, x, y, _ = place()
    for j, t in ((0, t0), (1, t1), (3, t3), (2, None)):
        for i in range(4):
            at = block_at(c, x, y, (4 - i) & 3, (4 - j) & 3)
            rows_s = pl.ds(pl.multiple_of(at * NS, NS), NS)
            rows_t = pl.ds(pl.multiple_of(at * NT, NT), NT)
            if t is None:
                hs[rows_s] = jnp.zeros((NS, TOK), BF16)
                ht[rows_t] = jnp.zeros((NT, TOK), BF16)
            else:
                hs[rows_s] = t[i, 0:NS]
                ht[rows_t] = t[i, NS : NS + NT]
    t_ref[:ROWS] = dot(wt[...], ht[...], ((1,), (0,)))
    t_ref[ROWS:] = dot(wto[...], ht[...], ((1,), (0,)))
    s_ref[:ROWS] = dot(ws[...], hs[...], ((1,), (0,)))
    s_ref[ROWS:] = dot(wso[...], hs[...], ((1,), (0,)))


def far_kernel(
    t2a, t2b, s_in, t_in, hs_in, ws, wso, wt, wto, es_ref, et_ref, st_ref, hs, pads
):
    _, c, x, y, _ = place()
    s_ref, t_ref = es_ref, et_ref
    hs[...] = hs_in[...]
    s_ref[...] = s_in[...]
    t_ref[...] = t_in[...]
    for i in range(4):
        line = t2a[i] if i < 2 else t2b[i - 2]
        at = block_at(c, x, y, (4 - i) & 3, 2)
        hs[pl.ds(pl.multiple_of(at * NS, NS), NS)] = line[0:NS]
        cols, first = window(at)
        pads[i] = jnp.zeros((WIDE, TOK), BF16)
        pads[i, pl.ds(first, NS)] = line[0:NS]
        cols_t = pl.ds(pl.multiple_of(at * NT, NT), NT)
        s_ref[:ROWS] += dot(ws[:, cols], pads[i], ((1,), (0,)))
        s_ref[ROWS:] += dot(wso[:, cols], pads[i], ((1,), (0,)))
        t_ref[:ROWS] += dot(wt[:, cols_t], line[NS:], ((1,), (0,)))
        t_ref[ROWS:] += dot(wto[:, cols_t], line[NS:], ((1,), (0,)))
    s, t = s_ref[...], t_ref[...]
    sm = jnp.max(s, axis=0, keepdims=True)
    tm = jnp.max(t, axis=0, keepdims=True)
    es, et = jnp.exp(s - sm), jnp.exp(t - tm)
    st_ref[0:1] = sm
    st_ref[1:2] = tm
    st_ref[2:3] = jnp.sum(es, axis=0, keepdims=True)
    st_ref[3:4] = jnp.sum(et, axis=0, keepdims=True)
    st_ref[4:5] = jnp.sum(et * (t - s), axis=0, keepdims=True)
    st_ref[5:8] = jnp.zeros((3, TOK), F32)
    es_ref[...] = es
    et_ref[...] = et


def vmem_call(kernel, name, outs, scratch, flops, *args):
    vmem = pl.BlockSpec(memory_space=pltpu.VMEM)
    return pl.pallas_call(
        kernel,
        out_shape=tuple(jax.ShapeDtypeStruct(*o) for o in outs),
        in_specs=[vmem] * len(args),
        out_specs=(vmem,) * len(outs),
        scratch_shapes=[pltpu.VMEM(*o) for o in scratch],
        compiler_params=pltpu.CompilerParams(vmem_limit_bytes=VMEM_LIMIT),
        cost_estimate=pl.CostEstimate(flops=flops, bytes_accessed=14_000_000, transcendentals=0),
        name=name,
    )(*args)


LOGITS = ((2 * ROWS, TOK), F32)
HIDDEN = ((DS, TOK), BF16)


def near_call(t0, t1, t3, *weights):
    flops = 2 * 2 * ROWS * TOK * (DS + DT)
    outs = (LOGITS, LOGITS, HIDDEN)
    return vmem_call(near_kernel, "near", outs, [((DT, TOK), BF16)], flops, t0, t1, t3, *weights)


def far_call(*args):
    flops = 2 * 2 * ROWS * TOK * (DS + DT) // 3
    outs = (LOGITS, LOGITS, ((8, TOK), F32), HIDDEN)
    return vmem_call(far_kernel, "far", outs, [((4, WIDE, TOK), BF16)], flops, *args)


CHUNK = 1280


def opposite_kernel(
    stats, local, weights, es_ref, et_ref, ws, wso, kl_ref, g_own, g_oth, o2a, o2b, part
):
    zl, c, x, y, _ = place()
    top = stats[0, 0:2]
    for i in range(1, 16):
        top = jnp.maximum(top, stats[i, 0:2])
    totals, cross = jnp.zeros((2, TOK), F32), jnp.zeros((1, TOK), F32)
    for i in range(16):
        scale = jnp.exp(stats[i, 0:2] - top)
        totals += stats[i, 2:4] * scale
        cross += stats[i, 4:5] * scale[1:2]
    kl = cross / totals[1:2] - top[1:2] - jnp.log(totals[1:2]) + top[0:1] + jnp.log(totals[0:1])
    kl_ref[...] = jnp.where(zl == 0, kl[:, :128], kl[:, 128:])
    weight = jnp.concatenate(
        [jnp.where(c == 0, weights[i : i + 1], weights[i + 1 : i + 2]) for i in (0, 2)], axis=1
    )
    coef = weight * (jnp.exp(local[0:2] - top) / totals)
    g = (es_ref[...] * coef[0:1] - et_ref[...] * coef[1:2]).astype(BF16)
    g_own[...] = g[:ROWS]
    g_oth[...] = g[ROWS:]
    for r in range(4):
        cols, first = window(block_at(c, x, y, r, 2))
        whole = dot(g[:ROWS], ws[:, cols], ((0,), (0,))) + dot(g[ROWS:], wso[:, cols], ((0,), (0,)))
        part[r] = whole.astype(BF16).T
        if r < 2:
            o2a[r] = part[r, pl.ds(first, NS)]
        else:
            o2b[r - 2] = part[r, pl.ds(first, NS)]


def rest_kernel(g_own, g_oth, ws, wso, o0, o1, o3, acc):
    _, c, x, y, _ = place()
    for n in range(DS // CHUNK):
        cols = slice(n * CHUNK, (n + 1) * CHUNK)
        part = dot(g_own[...], ws[:, cols], ((0,), (0,))) + dot(g_oth[...], wso[:, cols], ((0,), (0,)))
        acc[cols] = part.astype(BF16).T
    for k, o in ((0, o0), (1, o1), (3, o3)):
        for r in range(4):
            at = block_at(c, x, y, r, k)
            o[r] = acc[pl.ds(pl.multiple_of(at * NS, NS), NS)]


def opposite_call(*args):
    rows, half = ((ROWS, TOK), BF16), ((2, NS, TOK), BF16)
    outs = (((1, 128), F32), rows, rows, half, half)
    flops = 2 * 2 * ROWS * TOK * DS // 3
    return vmem_call(opposite_kernel, "opposite", outs, [((4, WIDE, TOK), BF16)], flops, *args)


def rest_call(*args):
    outs = (((4, NS, TOK), BF16),) * 3
    return vmem_call(rest_kernel, "rest", outs, [HIDDEN], 2 * 2 * ROWS * TOK * DS, *args)


def head_kernel(g_own, g_got, h_own, h_got, out):
    out[...] = (
        dot(g_own[...], h_own[...], ((1,), (1,))) + dot(g_got[...], h_got[...], ((1,), (1,)))
    ).astype(BF16)


def head_call(g_own, g_got, h_own, h_got):
    step = 640
    whole = pl.BlockSpec((ROWS, TOK), lambda i: (0, 0))
    some = pl.BlockSpec((step, TOK), lambda i: (i, 0))
    return pl.pallas_call(
        head_kernel,
        out_shape=jax.ShapeDtypeStruct((ROWS, DS), BF16),
        grid=(DS // step,),
        in_specs=[whole, whole, some, some],
        out_specs=pl.BlockSpec((ROWS, step), lambda i: (0, i)),
        compiler_params=pltpu.CompilerParams(vmem_limit_bytes=VMEM_LIMIT),
        cost_estimate=pl.CostEstimate(
            flops=2 * 2 * ROWS * TOK * DS, bytes_accessed=10_000_000, transcendentals=0
        ),
        name="head",
    )(g_own, g_got, h_own, h_got)


def merge(stats):
    top = stats[0][0:2]
    for s in stats[1:]:
        top = jnp.maximum(top, s[0:2])
    total = jnp.zeros_like(stats[0][2:5])
    for s in stats:
        scale = jnp.exp(s[0:2] - top)
        total = total + s[2:5] * jnp.concatenate([scale, scale[1:2]], axis=0)
    return jnp.concatenate([top, total, stats[0][5:8]], axis=0)


def per_device(student_hidden, teacher_hidden, student_head, teacher_head, row_weight):
    teacher_other = send(teacher_head, CORE)
    student_other = send(student_head, CORE)

    mine = jnp.concatenate([student_hidden.T, teacher_hidden.T], axis=0)
    copies = vmem_call(spread_kernel, "spread", [((8, 144, 128), BF16)], [], 1, mine)[0]
    along = lax.all_to_all(copies, ("zl", "zh"), 0, 0)
    block = vmem_call(weave_kernel, "weave", [((NS + NT, TOK), BF16)], [], 1, along)[0]
    line = jnp.stack((block,) + ring(block, FIRST))
    before, after = send(line, SECOND[1]), send(line, SECOND[3])
    far_low, far_high = send(before[:2], SECOND[1]), send(after[2:], SECOND[3])

    heads = (student_head, student_other, teacher_head, teacher_other)
    near = near_call(line, before, after, *heads)
    es, et, local, hidden_own = far_call(far_low, far_high, *near, *heads)
    stats = merge((local, send(local, PAIR)))
    stats = merge((stats,) + ring(stats, ZH))
    stats = lax.all_to_all(jnp.broadcast_to(stats, (16, 8, TOK)), ("x", "y"), 0, 0)
    kl_rows, g_own, g_oth, o2a, o2b = opposite_call(
        stats, local, row_weight.reshape(4, 128), es, et, student_head, student_other
    )
    low, high = send(o2a, SECOND[1]), send(o2b, SECOND[3])
    g_got, hidden_got = send(g_oth, CORE), send(hidden_own, CORE)
    low, high, g_got, hidden_got, o0, o1, o3 = lax.optimization_barrier(
        (low, high, g_got, hidden_got, *rest_call(g_own, g_oth, student_head, student_other))
    )
    o1 = jnp.concatenate([(o1[:2].astype(F32) + low.astype(F32)).astype(BF16), o1[2:]])
    o3 = jnp.concatenate([o3[:2], (o3[2:].astype(F32) + high.astype(F32)).astype(BF16)])
    r1, r3 = send(o1, SECOND[1]), send(o3, SECOND[3])
    head_grad = head_call(g_own, g_got, hidden_own, hidden_got)
    r1, r3, head_grad = lax.optimization_barrier((r1, r3, head_grad))

    sums = o0.astype(F32) + (r1.astype(F32) + r3.astype(F32))
    r1, r3, r2 = (send(sums[k].astype(BF16), FIRST[k]) for k in (1, 3, 2))
    sums = sums[0] + (r1.astype(F32) + r3.astype(F32)) + r2.astype(F32)
    sums = jnp.concatenate([sums[:, :128], sums[:, 128:]], axis=0).reshape(8, 80, 128)
    hidden_grad = jnp.sum(lax.all_to_all(sums, ("zl", "zh"), 0, 0), axis=0).T
    return (kl_rows.reshape(128), hidden_grad, head_grad)


def solution(mesh):
    fine = jax.sharding.Mesh(mesh.devices.reshape(2, 2, 4, 4, 4), AXES)
    pipe, vocab = AXES[:2], AXES[2:]
    placed = (P(pipe, vocab), P(pipe, vocab), P(AXES, None), P(AXES, None), P())
    return jax.shard_map(
        per_device,
        mesh=fine,
        in_specs=placed,
        out_specs=(P(pipe), P(pipe, vocab), P(AXES, None)),
        check_vma=False,
    )
```

```python
import jax
import jax.numpy as jnp
from jax import lax
from jax.experimental import pallas as pl
from jax.experimental.pallas import tpu as pltpu
from jax.sharding import PartitionSpec as P

DS, DT = 5120, 4096
ROWS = 384
TOK = 256
NS, NT = 320, 256
WIDE = 384
AXES = ("zl", "c", "x", "y", "zh")
F32, BF16 = jnp.float32, jnp.bfloat16
VMEM_LIMIT = 20 * 1024 * 1024


def coords(i):
    p, v = divmod(i, 64)
    return p >> 1, p & 1, v >> 4, (v >> 2) & 3, v & 3


def index(zl, c, x, y, zh):
    return (zl * 2 + c) * 64 + x * 16 + y * 4 + zh


def perm(move):
    return [(i, index(*move(*coords(i)))) for i in range(256)]


PAIR = perm(lambda zl, c, x, y, zh: (1 - zl, c, x, y, zh))
CORE = perm(lambda zl, c, x, y, zh: (zl, 1 - c, x, y, zh))
ZH = {k: perm(lambda zl, c, x, y, zh, k=k: (zl, c, x, y, zh ^ k)) for k in (1, 2, 3)}
FIRST = {
    k: perm(lambda zl, c, x, y, zh, k=k: (zl, c, x ^ (k * (1 - c)), y ^ (k * c), zh))
    for k in (1, 2, 3)
}
SECOND = {
    k: perm(lambda zl, c, x, y, zh, k=k: (zl, c, x ^ (k * c), y ^ (k * (1 - c)), zh))
    for k in (1, 2, 3)
}


def send(value, pairs):
    return lax.ppermute(value, AXES, pairs)


def ring(value, perms):
    got = {k: send(value, perms[k]) for k in (1, 3, 2)}
    return got[1], got[2], got[3]


def place():
    return tuple(lax.axis_index(a) for a in AXES)


def block_at(c, x, y, first, second):
    in_x = jnp.where(c == 0, first, second)
    in_y = jnp.where(c == 0, second, first)
    return (x ^ in_x) * 4 + (y ^ in_y)


def dot(a, b, dims):
    return lax.dot_general(a, b, (dims, ((), ())), preferred_element_type=F32)


def window(at):
    start = pl.multiple_of(((at * 5) >> 1) * 128, 128)
    return pl.ds(start, WIDE), pl.multiple_of((at & 1) * 64, 64)


def spread_kernel(mine, out):
    for i in range(8):
        out[i] = mine[...]


def weave_kernel(along, out):
    for zh in range(4):
        for zl in range(2):
            tokens = slice(zl * 128, (zl + 1) * 128)
            out[zh * 80 : (zh + 1) * 80, tokens] = along[zl * 4 + zh, 0:80]
            out[NS + zh * 64 : NS + (zh + 1) * 64, tokens] = along[zl * 4 + zh, 80:144]


def near_kernel(t0, t1, t3, ws, wso, wt, wto, s_ref, t_ref, hs, ht):
    _, c, x, y, _ = place()
    for j, t in ((0, t0), (1, t1), (3, t3), (2, None)):
        for i in range(4):
            at = block_at(c, x, y, i, j)
            rows_s = pl.ds(pl.multiple_of(at * NS, NS), NS)
            rows_t = pl.ds(pl.multiple_of(at * NT, NT), NT)
            if t is None:
                hs[rows_s] = jnp.zeros((NS, TOK), BF16)
                ht[rows_t] = jnp.zeros((NT, TOK), BF16)
            else:
                hs[rows_s] = t[i, 0:NS]
                ht[rows_t] = t[i, NS : NS + NT]
    t_ref[:ROWS] = dot(wt[...], ht[...], ((1,), (0,)))
    t_ref[ROWS:] = dot(wto[...], ht[...], ((1,), (0,)))
    s_ref[:ROWS] = dot(ws[...], hs[...], ((1,), (0,)))
    s_ref[ROWS:] = dot(wso[...], hs[...], ((1,), (0,)))


def far_kernel(
    t2a, t2b, s_in, t_in, hs_in, ws, wso, wt, wto, es_ref, et_ref, st_ref, hs, pads
):
    _, c, x, y, _ = place()
    s_ref, t_ref = es_ref, et_ref
    hs[...] = hs_in[...]
    s_ref[...] = s_in[...]
    t_ref[...] = t_in[...]
    for i in range(4):
        line = t2a[i] if i < 2 else t2b[i - 2]
        at = block_at(c, x, y, i, 2)
        hs[pl.ds(pl.multiple_of(at * NS, NS), NS)] = line[0:NS]
        cols, first = window(at)
        pads[i] = jnp.zeros((WIDE, TOK), BF16)
        pads[i, pl.ds(first, NS)] = line[0:NS]
        cols_t = pl.ds(pl.multiple_of(at * NT, NT), NT)
        s_ref[:ROWS] += dot(ws[:, cols], pads[i], ((1,), (0,)))
        s_ref[ROWS:] += dot(wso[:, cols], pads[i], ((1,), (0,)))
        t_ref[:ROWS] += dot(wt[:, cols_t], line[NS:], ((1,), (0,)))
        t_ref[ROWS:] += dot(wto[:, cols_t], line[NS:], ((1,), (0,)))
    s, t = s_ref[...], t_ref[...]
    sm = jnp.max(s, axis=0, keepdims=True)
    tm = jnp.max(t, axis=0, keepdims=True)
    es, et = jnp.exp(s - sm), jnp.exp(t - tm)
    st_ref[0:1] = sm
    st_ref[1:2] = tm
    st_ref[2:3] = jnp.sum(es, axis=0, keepdims=True)
    st_ref[3:4] = jnp.sum(et, axis=0, keepdims=True)
    st_ref[4:5] = jnp.sum(et * (t - s), axis=0, keepdims=True)
    st_ref[5:8] = jnp.zeros((3, TOK), F32)
    es_ref[...] = es
    et_ref[...] = et


def vmem_call(kernel, name, outs, scratch, flops, *args):
    vmem = pl.BlockSpec(memory_space=pltpu.VMEM)
    return pl.pallas_call(
        kernel,
        out_shape=tuple(jax.ShapeDtypeStruct(*o) for o in outs),
        in_specs=[vmem] * len(args),
        out_specs=(vmem,) * len(outs),
        scratch_shapes=[pltpu.VMEM(*o) for o in scratch],
        compiler_params=pltpu.CompilerParams(vmem_limit_bytes=VMEM_LIMIT),
        cost_estimate=pl.CostEstimate(flops=flops, bytes_accessed=14_000_000, transcendentals=0),
        name=name,
    )(*args)


LOGITS = ((2 * ROWS, TOK), F32)
HIDDEN = ((DS, TOK), BF16)


def near_call(t0, t1, t3, *weights):
    flops = 2 * 2 * ROWS * TOK * (DS + DT)
    outs = (LOGITS, LOGITS, HIDDEN)
    return vmem_call(near_kernel, "near", outs, [((DT, TOK), BF16)], flops, t0, t1, t3, *weights)


def far_call(*args):
    flops = 2 * 2 * ROWS * TOK * (DS + DT) // 3
    outs = (LOGITS, LOGITS, ((8, TOK), F32), HIDDEN)
    return vmem_call(far_kernel, "far", outs, [((4, WIDE, TOK), BF16)], flops, *args)


CHUNK = 1280


def opposite_kernel(
    stats, local, weights, es_ref, et_ref, ws, wso, kl_ref, g_own, g_oth, o2a, o2b, part
):
    zl, c, x, y, _ = place()
    top = stats[0, 0:2]
    for i in range(1, 16):
        top = jnp.maximum(top, stats[i, 0:2])
    totals, cross = jnp.zeros((2, TOK), F32), jnp.zeros((1, TOK), F32)
    for i in range(16):
        scale = jnp.exp(stats[i, 0:2] - top)
        totals += stats[i, 2:4] * scale
        cross += stats[i, 4:5] * scale[1:2]
    kl = cross / totals[1:2] - top[1:2] - jnp.log(totals[1:2]) + top[0:1] + jnp.log(totals[0:1])
    kl_ref[...] = jnp.where(zl == 0, kl[:, :128], kl[:, 128:])
    weight = jnp.concatenate(
        [jnp.where(c == 0, weights[i : i + 1], weights[i + 1 : i + 2]) for i in (0, 2)], axis=1
    )
    coef = weight * (jnp.exp(local[0:2] - top) / totals)
    g = (es_ref[...] * coef[0:1] - et_ref[...] * coef[1:2]).astype(BF16)
    g_own[...] = g[:ROWS]
    g_oth[...] = g[ROWS:]
    for r in range(4):
        cols, first = window(block_at(c, x, y, r, 2))
        whole = dot(g[:ROWS], ws[:, cols], ((0,), (0,))) + dot(g[ROWS:], wso[:, cols], ((0,), (0,)))
        part[r] = whole.astype(BF16).T
        if r < 2:
            o2a[r] = part[r, pl.ds(first, NS)]
        else:
            o2b[r - 2] = part[r, pl.ds(first, NS)]


def rest_kernel(g_own, g_oth, ws, wso, o0, o1, o3, acc):
    _, c, x, y, _ = place()
    for n in range(DS // CHUNK):
        cols = slice(n * CHUNK, (n + 1) * CHUNK)
        part = dot(g_own[...], ws[:, cols], ((0,), (0,))) + dot(g_oth[...], wso[:, cols], ((0,), (0,)))
        acc[cols] = part.astype(BF16).T
    for k, o in ((0, o0), (1, o1), (3, o3)):
        for r in range(4):
            at = block_at(c, x, y, r, k)
            o[r] = acc[pl.ds(pl.multiple_of(at * NS, NS), NS)]


def opposite_call(*args):
    rows, half = ((ROWS, TOK), BF16), ((2, NS, TOK), BF16)
    outs = (((1, 128), F32), rows, rows, half, half)
    flops = 2 * 2 * ROWS * TOK * DS // 3
    return vmem_call(opposite_kernel, "opposite", outs, [((4, WIDE, TOK), BF16)], flops, *args)


def rest_call(*args):
    outs = (((4, NS, TOK), BF16),) * 3
    return vmem_call(rest_kernel, "rest", outs, [HIDDEN], 2 * 2 * ROWS * TOK * DS, *args)


def head_kernel(g_own, g_got, h_own, h_got, out):
    out[...] = (
        dot(g_own[...], h_own[...], ((1,), (1,))) + dot(g_got[...], h_got[...], ((1,), (1,)))
    ).astype(BF16)


def head_call(g_own, g_got, h_own, h_got):
    step = 640
    whole = pl.BlockSpec((ROWS, TOK), lambda i: (0, 0))
    some = pl.BlockSpec((step, TOK), lambda i: (i, 0))
    return pl.pallas_call(
        head_kernel,
        out_shape=jax.ShapeDtypeStruct((ROWS, DS), BF16),
        grid=(DS // step,),
        in_specs=[whole, whole, some, some],
        out_specs=pl.BlockSpec((ROWS, step), lambda i: (0, i)),
        compiler_params=pltpu.CompilerParams(vmem_limit_bytes=VMEM_LIMIT),
        cost_estimate=pl.CostEstimate(
            flops=2 * 2 * ROWS * TOK * DS, bytes_accessed=10_000_000, transcendentals=0
        ),
        name="head",
    )(g_own, g_got, h_own, h_got)


def merge(stats):
    top = stats[0][0:2]
    for s in stats[1:]:
        top = jnp.maximum(top, s[0:2])
    total = jnp.zeros_like(stats[0][2:5])
    for s in stats:
        scale = jnp.exp(s[0:2] - top)
        total = total + s[2:5] * jnp.concatenate([scale, scale[1:2]], axis=0)
    return jnp.concatenate([top, total, stats[0][5:8]], axis=0)


def per_device(student_hidden, teacher_hidden, student_head, teacher_head, row_weight):
    teacher_other = send(teacher_head, CORE)
    student_other = send(student_head, CORE)

    mine = jnp.concatenate([student_hidden.T, teacher_hidden.T], axis=0)
    copies = vmem_call(spread_kernel, "spread", [((8, 144, 128), BF16)], [], 1, mine)[0]
    along = lax.all_to_all(copies, ("zl", "zh"), 0, 0)
    block = vmem_call(weave_kernel, "weave", [((NS + NT, TOK), BF16)], [], 1, along)[0]
    line = jnp.stack((block,) + ring(block, FIRST))
    before, after = send(line, SECOND[1]), send(line, SECOND[3])
    far_low, far_high = send(after[:2], SECOND[1]), send(before[2:], SECOND[3])

    heads = (student_head, student_other, teacher_head, teacher_other)
    near = near_call(line, before, after, *heads)
    es, et, local, hidden_own = far_call(far_low, far_high, *near, *heads)
    stats = merge((local, send(local, PAIR)))
    stats = merge((stats,) + ring(stats, ZH))
    stats = lax.all_to_all(jnp.broadcast_to(stats, (16, 8, TOK)), ("x", "y"), 0, 0)
    kl_rows, g_own, g_oth, o2a, o2b = opposite_call(
        stats, local, row_weight.reshape(4, 128), es, et, student_head, student_other
    )
    low, high = send(o2a, SECOND[1]), send(o2b, SECOND[3])
    g_got, hidden_got = send(g_oth, CORE), send(hidden_own, CORE)
    low, high, g_got, hidden_got, o0, o1, o3 = lax.optimization_barrier(
        (low, high, g_got, hidden_got, *rest_call(g_own, g_oth, student_head, student_other))
    )
    o3 = jnp.concatenate([(o3[:2].astype(F32) + low.astype(F32)).astype(BF16), o3[2:]])
    o1 = jnp.concatenate([o1[:2], (o1[2:].astype(F32) + high.astype(F32)).astype(BF16)])
    r1, r3 = send(o1, SECOND[1]), send(o3, SECOND[3])
    head_grad = head_call(g_own, g_got, hidden_own, hidden_got)
    r1, r3, head_grad = lax.optimization_barrier((r1, r3, head_grad))

    sums = o0.astype(F32) + (r1.astype(F32) + r3.astype(F32))
    r1, r3, r2 = (send(sums[k].astype(BF16), FIRST[k]) for k in (1, 3, 2))
    sums = sums[0] + (r1.astype(F32) + r3.astype(F32)) + r2.astype(F32)
    sums = jnp.concatenate([sums[:, :128], sums[:, 128:]], axis=0).reshape(8, 80, 128)
    hidden_grad = jnp.sum(lax.all_to_all(sums, ("zl", "zh"), 0, 0), axis=0).T
    return (kl_rows.reshape(128), hidden_grad, head_grad)


def solution(mesh):
    fine = jax.sharding.Mesh(mesh.devices.reshape(2, 2, 4, 4, 4), AXES)
    pipe, vocab = AXES[:2], AXES[2:]
    placed = (P(pipe, vocab), P(pipe, vocab), P(AXES, None), P(AXES, None), P())
    return jax.shard_map(
        per_device,
        mesh=fine,
        in_specs=placed,
        out_specs=(P(pipe), P(pipe, vocab), P(AXES, None)),
        check_vma=False,
    )
```

```python
import jax
import jax.numpy as jnp
from jax import lax
from jax.experimental import pallas as pl
from jax.experimental.pallas import tpu as pltpu
from jax.sharding import PartitionSpec as P

DS, DT = 5120, 4096
ROWS = 384
TOK = 256
NS, NT = 320, 256
WIDE = 384
AXES = ("zl", "c", "x", "y", "zh")
F32, BF16 = jnp.float32, jnp.bfloat16
VMEM_LIMIT = 20 * 1024 * 1024


def coords(i):
    p, v = divmod(i, 64)
    return p >> 1, p & 1, v >> 4, (v >> 2) & 3, v & 3


def index(zl, c, x, y, zh):
    return (zl * 2 + c) * 64 + x * 16 + y * 4 + zh


def perm(move):
    return [(i, index(*move(*coords(i)))) for i in range(256)]


PAIR = perm(lambda zl, c, x, y, zh: (1 - zl, c, x, y, zh))
CORE = perm(lambda zl, c, x, y, zh: (zl, 1 - c, x, y, zh))
ZH = {k: perm(lambda zl, c, x, y, zh, k=k: (zl, c, x, y, zh ^ k)) for k in (1, 2, 3)}
FIRST = {
    k: perm(lambda zl, c, x, y, zh, k=k: (zl, c, x ^ (k * (1 - c)), y ^ (k * c), zh))
    for k in (1, 2, 3)
}
SECOND = {
    k: perm(lambda zl, c, x, y, zh, k=k: (zl, c, x ^ (k * c), y ^ (k * (1 - c)), zh))
    for k in (1, 2, 3)
}


def send(value, pairs):
    return lax.ppermute(value, AXES, pairs)


def ring(value, perms):
    got = {k: send(value, perms[k]) for k in (1, 3, 2)}
    return got[1], got[2], got[3]


def place():
    return tuple(lax.axis_index(a) for a in AXES)


def block_at(c, x, y, first, second):
    in_x = jnp.where(c == 0, first, second)
    in_y = jnp.where(c == 0, second, first)
    return (x ^ in_x) * 4 + (y ^ in_y)


def dot(a, b, dims):
    return lax.dot_general(a, b, (dims, ((), ())), preferred_element_type=F32)


def window(at):
    start = pl.multiple_of(((at * 5) >> 1) * 128, 128)
    return pl.ds(start, WIDE), pl.multiple_of((at & 1) * 64, 64)


def beside_kernel(mine, pair, out):
    first = lax.axis_index("zl") == 0
    out[:, :128] = jnp.where(first, mine[...], pair[...])
    out[:, 128:] = jnp.where(first, pair[...], mine[...])


def weave_kernel(r0, r1, r2, r3, out):
    zh = lax.axis_index("zh")
    for k, r in enumerate((r0, r1, r2, r3)):
        out[pl.ds(pl.multiple_of((zh ^ k) * 80, 16), 80)] = r[0:80]
        out[pl.ds(pl.multiple_of(NS + (zh ^ k) * 64, 64), 64)] = r[80:144]


def near_kernel(t0, t1, t3, ws, wso, wt, wto, s_ref, t_ref, hs, ht):
    _, c, x, y, _ = place()
    for j, t in ((0, t0), (1, t1), (3, t3), (2, None)):
        for i in range(4):
            at = block_at(c, x, y, i, j)
            rows_s = pl.ds(pl.multiple_of(at * NS, NS), NS)
            rows_t = pl.ds(pl.multiple_of(at * NT, NT), NT)
            if t is None:
                hs[rows_s] = jnp.zeros((NS, TOK), BF16)
                ht[rows_t] = jnp.zeros((NT, TOK), BF16)
            else:
                hs[rows_s] = t[i, 0:NS]
                ht[rows_t] = t[i, NS : NS + NT]
    t_ref[:ROWS] = dot(wt[...], ht[...], ((1,), (0,)))
    t_ref[ROWS:] = dot(wto[...], ht[...], ((1,), (0,)))
    s_ref[:ROWS] = dot(ws[...], hs[...], ((1,), (0,)))
    s_ref[ROWS:] = dot(wso[...], hs[...], ((1,), (0,)))


def far_kernel(
    t2a, t2b, s_in, t_in, hs_in, ws, wso, wt, wto, es_ref, et_ref, st_ref, hs, pads
):
    _, c, x, y, _ = place()
    s_ref, t_ref = es_ref, et_ref
    hs[...] = hs_in[...]
    s_ref[...] = s_in[...]
    t_ref[...] = t_in[...]
    for i in range(4):
        line = t2a[i] if i < 2 else t2b[i - 2]
        at = block_at(c, x, y, i, 2)
        hs[pl.ds(pl.multiple_of(at * NS, NS), NS)] = line[0:NS]
        cols, first = window(at)
        pads[i] = jnp.zeros((WIDE, TOK), BF16)
        pads[i, pl.ds(first, NS)] = line[0:NS]
        cols_t = pl.ds(pl.multiple_of(at * NT, NT), NT)
        s_ref[:ROWS] += dot(ws[:, cols], pads[i], ((1,), (0,)))
        s_ref[ROWS:] += dot(wso[:, cols], pads[i], ((1,), (0,)))
        t_ref[:ROWS] += dot(wt[:, cols_t], line[NS:], ((1,), (0,)))
        t_ref[ROWS:] += dot(wto[:, cols_t], line[NS:], ((1,), (0,)))
    s, t = s_ref[...], t_ref[...]
    sm = jnp.max(s, axis=0, keepdims=True)
    tm = jnp.max(t, axis=0, keepdims=True)
    es, et = jnp.exp(s - sm), jnp.exp(t - tm)
    st_ref[0:1] = sm
    st_ref[1:2] = tm
    st_ref[2:3] = jnp.sum(es, axis=0, keepdims=True)
    st_ref[3:4] = jnp.sum(et, axis=0, keepdims=True)
    st_ref[4:5] = jnp.sum(et * (t - s), axis=0, keepdims=True)
    st_ref[5:8] = jnp.zeros((3, TOK), F32)
    es_ref[...] = es
    et_ref[...] = et


def vmem_call(kernel, name, outs, scratch, flops, *args):
    vmem = pl.BlockSpec(memory_space=pltpu.VMEM)
    return pl.pallas_call(
        kernel,
        out_shape=tuple(jax.ShapeDtypeStruct(*o) for o in outs),
        in_specs=[vmem] * len(args),
        out_specs=(vmem,) * len(outs),
        scratch_shapes=[pltpu.VMEM(*o) for o in scratch],
        compiler_params=pltpu.CompilerParams(vmem_limit_bytes=VMEM_LIMIT),
        cost_estimate=pl.CostEstimate(flops=flops, bytes_accessed=14_000_000, transcendentals=0),
        name=name,
    )(*args)


LOGITS = ((2 * ROWS, TOK), F32)
HIDDEN = ((DS, TOK), BF16)


def near_call(t0, t1, t3, *weights):
    flops = 2 * 2 * ROWS * TOK * (DS + DT)
    outs = (LOGITS, LOGITS, HIDDEN)
    return vmem_call(near_kernel, "near", outs, [((DT, TOK), BF16)], flops, t0, t1, t3, *weights)


def far_call(*args):
    flops = 2 * 2 * ROWS * TOK * (DS + DT) // 3
    outs = (LOGITS, LOGITS, ((8, TOK), F32), HIDDEN)
    return vmem_call(far_kernel, "far", outs, [((4, WIDE, TOK), BF16)], flops, *args)


CHUNK = 1280


def opposite_kernel(
    stats, local, weights, es_ref, et_ref, ws, wso, kl_ref, g_own, g_oth, o2a, o2b, part
):
    zl, c, x, y, _ = place()
    top = stats[0, 0:2]
    for i in range(1, 16):
        top = jnp.maximum(top, stats[i, 0:2])
    totals, cross = jnp.zeros((2, TOK), F32), jnp.zeros((1, TOK), F32)
    for i in range(16):
        scale = jnp.exp(stats[i, 0:2] - top)
        totals += stats[i, 2:4] * scale
        cross += stats[i, 4:5] * scale[1:2]
    kl = cross / totals[1:2] - top[1:2] - jnp.log(totals[1:2]) + top[0:1] + jnp.log(totals[0:1])
    kl_ref[...] = jnp.where(zl == 0, kl[:, :128], kl[:, 128:])
    weight = jnp.concatenate(
        [jnp.where(c == 0, weights[i : i + 1], weights[i + 1 : i + 2]) for i in (0, 2)], axis=1
    )
    coef = weight * (jnp.exp(local[0:2] - top) / totals)
    g = (es_ref[...] * coef[0:1] - et_ref[...] * coef[1:2]).astype(BF16)
    g_own[...] = g[:ROWS]
    g_oth[...] = g[ROWS:]
    for r in range(4):
        cols, first = window(block_at(c, x, y, r, 2))
        whole = dot(g[:ROWS], ws[:, cols], ((0,), (0,))) + dot(g[ROWS:], wso[:, cols], ((0,), (0,)))
        part[r] = whole.astype(BF16).T
        if r < 2:
            o2a[r] = part[r, pl.ds(first, NS)]
        else:
            o2b[r - 2] = part[r, pl.ds(first, NS)]


def rest_kernel(g_own, g_oth, ws, wso, o0, o1, o3, acc):
    _, c, x, y, _ = place()
    for n in range(DS // CHUNK):
        cols = slice(n * CHUNK, (n + 1) * CHUNK)
        part = dot(g_own[...], ws[:, cols], ((0,), (0,))) + dot(g_oth[...], wso[:, cols], ((0,), (0,)))
        acc[cols] = part.astype(BF16).T
    for k, o in ((0, o0), (1, o1), (3, o3)):
        for r in range(4):
            at = block_at(c, x, y, r, k)
            o[r] = acc[pl.ds(pl.multiple_of(at * NS, NS), NS)]


def opposite_call(*args):
    rows, half = ((ROWS, TOK), BF16), ((2, NS, TOK), BF16)
    outs = (((1, 128), F32), rows, rows, half, half)
    flops = 2 * 2 * ROWS * TOK * DS // 3
    return vmem_call(opposite_kernel, "opposite", outs, [((4, WIDE, TOK), BF16)], flops, *args)


def rest_call(*args):
    outs = (((4, NS, TOK), BF16),) * 3
    return vmem_call(rest_kernel, "rest", outs, [HIDDEN], 2 * 2 * ROWS * TOK * DS, *args)


def head_kernel(g_own, g_got, h_own, h_got, out):
    out[...] = (
        dot(g_own[...], h_own[...], ((1,), (1,))) + dot(g_got[...], h_got[...], ((1,), (1,)))
    ).astype(BF16)


def head_call(g_own, g_got, h_own, h_got):
    step = 640
    whole = pl.BlockSpec((ROWS, TOK), lambda i: (0, 0))
    some = pl.BlockSpec((step, TOK), lambda i: (i, 0))
    return pl.pallas_call(
        head_kernel,
        out_shape=jax.ShapeDtypeStruct((ROWS, DS), BF16),
        grid=(DS // step,),
        in_specs=[whole, whole, some, some],
        out_specs=pl.BlockSpec((ROWS, step), lambda i: (0, i)),
        compiler_params=pltpu.CompilerParams(vmem_limit_bytes=VMEM_LIMIT),
        cost_estimate=pl.CostEstimate(
            flops=2 * 2 * ROWS * TOK * DS, bytes_accessed=10_000_000, transcendentals=0
        ),
        name="head",
    )(g_own, g_got, h_own, h_got)


def merge(stats):
    top = stats[0][0:2]
    for s in stats[1:]:
        top = jnp.maximum(top, s[0:2])
    total = jnp.zeros_like(stats[0][2:5])
    for s in stats:
        scale = jnp.exp(s[0:2] - top)
        total = total + s[2:5] * jnp.concatenate([scale, scale[1:2]], axis=0)
    return jnp.concatenate([top, total, stats[0][5:8]], axis=0)


def per_device(student_hidden, teacher_hidden, student_head, teacher_head, row_weight):
    teacher_other = send(teacher_head, CORE)
    student_other = send(student_head, CORE)

    mine = jnp.concatenate([student_hidden.T, teacher_hidden.T], axis=0)
    both = vmem_call(
        beside_kernel, "beside", [((144, TOK), BF16)], [], 1, mine, send(mine, PAIR)
    )[0]
    block = vmem_call(
        weave_kernel, "weave", [((NS + NT, TOK), BF16)], [], 1, both, *ring(both, ZH)
    )[0]
    line = jnp.stack((block,) + ring(block, FIRST))
    before, after = send(line, SECOND[1]), send(line, SECOND[3])
    far_low, far_high = send(after[:2], SECOND[1]), send(before[2:], SECOND[3])

    heads = (student_head, student_other, teacher_head, teacher_other)
    near = near_call(line, before, after, *heads)
    es, et, local, hidden_own = far_call(far_low, far_high, *near, *heads)
    stats = merge((local, send(local, PAIR)))
    stats = merge((stats,) + ring(stats, ZH))
    stats = lax.all_to_all(jnp.broadcast_to(stats, (16, 8, TOK)), ("x", "y"), 0, 0)
    kl_rows, g_own, g_oth, o2a, o2b = opposite_call(
        stats, local, row_weight.reshape(4, 128), es, et, student_head, student_other
    )
    low, high = send(o2a, SECOND[1]), send(o2b, SECOND[3])
    g_got, hidden_got = send(g_oth, CORE), send(hidden_own, CORE)
    low, high, g_got, hidden_got, o0, o1, o3 = lax.optimization_barrier(
        (low, high, g_got, hidden_got, *rest_call(g_own, g_oth, student_head, student_other))
    )
    o3 = jnp.concatenate([(o3[:2].astype(F32) + low.astype(F32)).astype(BF16), o3[2:]])
    o1 = jnp.concatenate([o1[:2], (o1[2:].astype(F32) + high.astype(F32)).astype(BF16)])
    r1, r3 = send(o1, SECOND[1]), send(o3, SECOND[3])
    head_grad = head_call(g_own, g_got, hidden_own, hidden_got)
    r1, r3, head_grad = lax.optimization_barrier((r1, r3, head_grad))

    sums = o0.astype(F32) + (r1.astype(F32) + r3.astype(F32))
    r1, r3, r2 = (send(sums[k].astype(BF16), FIRST[k]) for k in (1, 3, 2))
    sums = sums[0] + (r1.astype(F32) + r3.astype(F32)) + r2.astype(F32)
    sums = jnp.concatenate([sums[:, :128], sums[:, 128:]], axis=0).reshape(8, 80, 128)
    hidden_grad = jnp.sum(lax.all_to_all(sums, ("zl", "zh"), 0, 0), axis=0).T
    return (kl_rows.reshape(128), hidden_grad, head_grad)


def solution(mesh):
    fine = jax.sharding.Mesh(mesh.devices.reshape(2, 2, 4, 4, 4), AXES)
    pipe, vocab = AXES[:2], AXES[2:]
    placed = (P(pipe, vocab), P(pipe, vocab), P(AXES, None), P(AXES, None), P())
    return jax.shard_map(
        per_device,
        mesh=fine,
        in_specs=placed,
        out_specs=(P(pipe), P(pipe, vocab), P(AXES, None)),
        check_vma=False,
    )
```

```python
import jax
import jax.numpy as jnp
from jax import lax
from jax.experimental import pallas as pl
from jax.experimental.pallas import tpu as pltpu
from jax.sharding import PartitionSpec as P

DS, DT = 5120, 4096
ROWS = 384
TOK = 256
NS, NT = 320, 256
WIDE = 384
AXES = ("zl", "c", "x", "y", "zh")
F32, BF16 = jnp.float32, jnp.bfloat16
VMEM_LIMIT = 20 * 1024 * 1024


def coords(i):
    p, v = divmod(i, 64)
    return p >> 1, p & 1, v >> 4, (v >> 2) & 3, v & 3


def index(zl, c, x, y, zh):
    return (zl * 2 + c) * 64 + x * 16 + y * 4 + zh


def perm(move):
    return [(i, index(*move(*coords(i)))) for i in range(256)]


PAIR = perm(lambda zl, c, x, y, zh: (1 - zl, c, x, y, zh))
CORE = perm(lambda zl, c, x, y, zh: (zl, 1 - c, x, y, zh))
ZH = {k: perm(lambda zl, c, x, y, zh, k=k: (zl, c, x, y, zh ^ k)) for k in (1, 2, 3)}
FIRST = {
    k: perm(lambda zl, c, x, y, zh, k=k: (zl, c, x ^ (k * (1 - c)), y ^ (k * c), zh))
    for k in (1, 2, 3)
}
SECOND = {
    k: perm(lambda zl, c, x, y, zh, k=k: (zl, c, x ^ (k * c), y ^ (k * (1 - c)), zh))
    for k in (1, 2, 3)
}


def send(value, pairs):
    return lax.ppermute(value, AXES, pairs)


def ring(value, perms):
    got = {k: send(value, perms[k]) for k in (1, 3, 2)}
    return got[1], got[2], got[3]


def place():
    return tuple(lax.axis_index(a) for a in AXES)


def block_at(c, x, y, first, second):
    in_x = jnp.where(c == 0, first, second)
    in_y = jnp.where(c == 0, second, first)
    return (x ^ in_x) * 4 + (y ^ in_y)


def dot(a, b, dims):
    return lax.dot_general(a, b, (dims, ((), ())), preferred_element_type=F32)


def window(at):
    start = pl.multiple_of(((at * 5) >> 1) * 128, 128)
    return pl.ds(start, WIDE), pl.multiple_of((at & 1) * 64, 64)


def spread_kernel(mine, out):
    for i in range(8):
        out[i] = mine[...]


def weave_kernel(along, out):
    for zh in range(4):
        for zl in range(2):
            tokens = slice(zl * 128, (zl + 1) * 128)
            out[zh * 80 : (zh + 1) * 80, tokens] = along[zl * 4 + zh, 0:80]
            out[NS + zh * 64 : NS + (zh + 1) * 64, tokens] = along[zl * 4 + zh, 80:144]


def near_kernel(t0, t1, t3, ws, wso, wt, wto, s_ref, t_ref, hs, ht):
    _, c, x, y, _ = place()
    for j, t in ((0, t0), (1, t1), (3, t3), (2, None)):
        for i in range(4):
            at = block_at(c, x, y, i, j)
            rows_s = pl.ds(pl.multiple_of(at * NS, NS), NS)
            rows_t = pl.ds(pl.multiple_of(at * NT, NT), NT)
            if t is None:
                hs[rows_s] = jnp.zeros((NS, TOK), BF16)
                ht[rows_t] = jnp.zeros((NT, TOK), BF16)
            else:
                hs[rows_s] = t[i, 0:NS]
                ht[rows_t] = t[i, NS : NS + NT]
    t_ref[:ROWS] = dot(wt[...], ht[...], ((1,), (0,)))
    t_ref[ROWS:] = dot(wto[...], ht[...], ((1,), (0,)))
    s_ref[:ROWS] = dot(ws[...], hs[...], ((1,), (0,)))
    s_ref[ROWS:] = dot(wso[...], hs[...], ((1,), (0,)))


def far_kernel(
    t2a, t2b, s_in, t_in, hs_in, ws, wso, wt, wto, es_ref, et_ref, st_ref, hs, pads
):
    _, c, x, y, _ = place()
    s_ref, t_ref = es_ref, et_ref
    hs[...] = hs_in[...]
    s_ref[...] = s_in[...]
    t_ref[...] = t_in[...]
    for i in range(4):
        line = t2a[i] if i < 2 else t2b[i - 2]
        at = block_at(c, x, y, i, 2)
        hs[pl.ds(pl.multiple_of(at * NS, NS), NS)] = line[0:NS]
        cols, first = window(at)
        pads[i] = jnp.zeros((WIDE, TOK), BF16)
        pads[i, pl.ds(first, NS)] = line[0:NS]
        cols_t = pl.ds(pl.multiple_of(at * NT, NT), NT)
        s_ref[:ROWS] += dot(ws[:, cols], pads[i], ((1,), (0,)))
        s_ref[ROWS:] += dot(wso[:, cols], pads[i], ((1,), (0,)))
        t_ref[:ROWS] += dot(wt[:, cols_t], line[NS:], ((1,), (0,)))
        t_ref[ROWS:] += dot(wto[:, cols_t], line[NS:], ((1,), (0,)))
    s, t = s_ref[...], t_ref[...]
    sm = jnp.max(s, axis=0, keepdims=True)
    tm = jnp.max(t, axis=0, keepdims=True)
    es, et = jnp.exp(s - sm), jnp.exp(t - tm)
    st_ref[0:1] = sm
    st_ref[1:2] = tm
    st_ref[2:3] = jnp.sum(es, axis=0, keepdims=True)
    st_ref[3:4] = jnp.sum(et, axis=0, keepdims=True)
    st_ref[4:5] = jnp.sum(et * (t - s), axis=0, keepdims=True)
    st_ref[5:8] = jnp.zeros((3, TOK), F32)
    es_ref[...] = es
    et_ref[...] = et


def vmem_call(kernel, name, outs, scratch, flops, *args):
    vmem = pl.BlockSpec(memory_space=pltpu.VMEM)
    return pl.pallas_call(
        kernel,
        out_shape=tuple(jax.ShapeDtypeStruct(*o) for o in outs),
        in_specs=[vmem] * len(args),
        out_specs=(vmem,) * len(outs),
        scratch_shapes=[pltpu.VMEM(*o) for o in scratch],
        compiler_params=pltpu.CompilerParams(vmem_limit_bytes=VMEM_LIMIT),
        cost_estimate=pl.CostEstimate(flops=flops, bytes_accessed=14_000_000, transcendentals=0),
        name=name,
    )(*args)


LOGITS = ((2 * ROWS, TOK), F32)
HIDDEN = ((DS, TOK), BF16)


def near_call(t0, t1, t3, *weights):
    flops = 2 * 2 * ROWS * TOK * (DS + DT)
    outs = (LOGITS, LOGITS, HIDDEN)
    return vmem_call(near_kernel, "near", outs, [((DT, TOK), BF16)], flops, t0, t1, t3, *weights)


def far_call(*args):
    flops = 2 * 2 * ROWS * TOK * (DS + DT) // 3
    outs = (LOGITS, LOGITS, ((8, TOK), F32), HIDDEN)
    return vmem_call(far_kernel, "far", outs, [((4, WIDE, TOK), BF16)], flops, *args)


CHUNK = 1280


def opposite_kernel(
    stats, local, weights, es_ref, et_ref, ws, wso, kl_ref, g_own, g_oth, o2, part
):
    zl, c, x, y, _ = place()
    top = stats[0, 0:2]
    for i in range(1, 16):
        top = jnp.maximum(top, stats[i, 0:2])
    totals, cross = jnp.zeros((2, TOK), F32), jnp.zeros((1, TOK), F32)
    for i in range(16):
        scale = jnp.exp(stats[i, 0:2] - top)
        totals += stats[i, 2:4] * scale
        cross += stats[i, 4:5] * scale[1:2]
    kl = cross / totals[1:2] - top[1:2] - jnp.log(totals[1:2]) + top[0:1] + jnp.log(totals[0:1])
    kl_ref[...] = jnp.where(zl == 0, kl[:, :128], kl[:, 128:])
    weight = jnp.concatenate(
        [jnp.where(c == 0, weights[i : i + 1], weights[i + 1 : i + 2]) for i in (0, 2)], axis=1
    )
    coef = weight * (jnp.exp(local[0:2] - top) / totals)
    g = (es_ref[...] * coef[0:1] - et_ref[...] * coef[1:2]).astype(BF16)
    g_own[...] = g[:ROWS]
    g_oth[...] = g[ROWS:]
    for r in range(4):
        cols, first = window(block_at(c, x, y, r, 2))
        whole = dot(g[:ROWS], ws[:, cols], ((0,), (0,))) + dot(g[ROWS:], wso[:, cols], ((0,), (0,)))
        part[r] = whole.astype(BF16).T
        o2[r] = part[r, pl.ds(first, NS)]


def rest_kernel(g_own, g_oth, ws, wso, o0, o1, o3, acc):
    _, c, x, y, _ = place()
    for n in range(DS // CHUNK):
        cols = slice(n * CHUNK, (n + 1) * CHUNK)
        part = dot(g_own[...], ws[:, cols], ((0,), (0,))) + dot(g_oth[...], wso[:, cols], ((0,), (0,)))
        acc[cols] = part.astype(BF16).T
    for k, o in ((0, o0), (1, o1), (3, o3)):
        for r in range(4):
            at = block_at(c, x, y, r, k)
            o[r] = acc[pl.ds(pl.multiple_of(at * NS, NS), NS)]


def opposite_call(*args):
    rows = ((ROWS, TOK), BF16)
    outs = (((1, 128), F32), rows, rows, ((4, NS, TOK), BF16))
    flops = 2 * 2 * ROWS * TOK * DS // 3
    return vmem_call(opposite_kernel, "opposite", outs, [((4, WIDE, TOK), BF16)], flops, *args)


def rest_call(*args):
    outs = (((4, NS, TOK), BF16),) * 3
    return vmem_call(rest_kernel, "rest", outs, [HIDDEN], 2 * 2 * ROWS * TOK * DS, *args)


def head_kernel(g_own, g_got, h_own, h_got, out):
    out[...] = (
        dot(g_own[...], h_own[...], ((1,), (1,))) + dot(g_got[...], h_got[...], ((1,), (1,)))
    ).astype(BF16)


def head_call(g_own, g_got, h_own, h_got):
    step = 640
    whole = pl.BlockSpec((ROWS, TOK), lambda i: (0, 0))
    some = pl.BlockSpec((step, TOK), lambda i: (i, 0))
    return pl.pallas_call(
        head_kernel,
        out_shape=jax.ShapeDtypeStruct((ROWS, DS), BF16),
        grid=(DS // step,),
        in_specs=[whole, whole, some, some],
        out_specs=pl.BlockSpec((ROWS, step), lambda i: (0, i)),
        compiler_params=pltpu.CompilerParams(vmem_limit_bytes=VMEM_LIMIT),
        cost_estimate=pl.CostEstimate(
            flops=2 * 2 * ROWS * TOK * DS, bytes_accessed=10_000_000, transcendentals=0
        ),
        name="head",
    )(g_own, g_got, h_own, h_got)


def merge(stats):
    top = stats[0][0:2]
    for s in stats[1:]:
        top = jnp.maximum(top, s[0:2])
    total = jnp.zeros_like(stats[0][2:5])
    for s in stats:
        scale = jnp.exp(s[0:2] - top)
        total = total + s[2:5] * jnp.concatenate([scale, scale[1:2]], axis=0)
    return jnp.concatenate([top, total, stats[0][5:8]], axis=0)


def per_device(student_hidden, teacher_hidden, student_head, teacher_head, row_weight):
    teacher_other = send(teacher_head, CORE)
    student_other = send(student_head, CORE)

    mine = jnp.concatenate([student_hidden.T, teacher_hidden.T], axis=0)
    copies = vmem_call(spread_kernel, "spread", [((8, 144, 128), BF16)], [], 1, mine)[0]
    along = lax.all_to_all(copies, ("zl", "zh"), 0, 0)
    block = vmem_call(weave_kernel, "weave", [((NS + NT, TOK), BF16)], [], 1, along)[0]
    line = jnp.stack((block,) + ring(block, FIRST))
    before, after = send(line, SECOND[1]), send(line, SECOND[3])
    far_low, far_high = send(after[:2], SECOND[1]), send(before[2:], SECOND[3])

    heads = (student_head, student_other, teacher_head, teacher_other)
    near = near_call(line, before, after, *heads)
    es, et, local, hidden_own = far_call(far_low, far_high, *near, *heads)
    stats = merge((local, send(local, PAIR)))
    stats = merge((stats,) + ring(stats, ZH))
    stats = lax.all_to_all(jnp.broadcast_to(stats, (16, 8, TOK)), ("x", "y"), 0, 0)
    kl_rows, g_own, g_oth, o2 = opposite_call(
        stats, local, row_weight.reshape(4, 128), es, et, student_head, student_other
    )
    r2 = send(o2, SECOND[2])
    g_got, hidden_got = send(g_oth, CORE), send(hidden_own, CORE)
    g_got, hidden_got, o0, o1, o3 = lax.optimization_barrier(
        (g_got, hidden_got, *rest_call(g_own, g_oth, student_head, student_other))
    )
    r1, r3 = send(o1, SECOND[1]), send(o3, SECOND[3])
    head_grad = head_call(g_own, g_got, hidden_own, hidden_got)
    r1, r2, r3, head_grad = lax.optimization_barrier((r1, r2, r3, head_grad))

    sums = o0.astype(F32) + (r1.astype(F32) + r3.astype(F32)) + r2.astype(F32)
    r1, r3, r2 = (send(sums[k].astype(BF16), FIRST[k]) for k in (1, 3, 2))
    sums = sums[0] + (r1.astype(F32) + r3.astype(F32)) + r2.astype(F32)
    sums = jnp.concatenate([sums[:, :128], sums[:, 128:]], axis=0).reshape(8, 80, 128)
    hidden_grad = jnp.sum(lax.all_to_all(sums, ("zl", "zh"), 0, 0), axis=0).T
    return (kl_rows.reshape(128), hidden_grad, head_grad)


def solution(mesh):
    fine = jax.sharding.Mesh(mesh.devices.reshape(2, 2, 4, 4, 4), AXES)
    pipe, vocab = AXES[:2], AXES[2:]
    placed = (P(pipe, vocab), P(pipe, vocab), P(AXES, None), P(AXES, None), P())
    return jax.shard_map(
        per_device,
        mesh=fine,
        in_specs=placed,
        out_specs=(P(pipe), P(pipe, vocab), P(AXES, None)),
        check_vma=False,
    )
```

```python
import jax
import jax.numpy as jnp
from jax import lax
from jax.experimental import pallas as pl
from jax.experimental.pallas import tpu as pltpu
from jax.sharding import PartitionSpec as P

DS, DT = 5120, 4096
ROWS = 384
TOK = 256
NS, NT = 320, 256
WIDE = 384
AXES = ("zl", "c", "x", "y", "zh")
F32, BF16 = jnp.float32, jnp.bfloat16
VMEM_LIMIT = 20 * 1024 * 1024


def coords(i):
    p, v = divmod(i, 64)
    return p >> 1, p & 1, v >> 4, (v >> 2) & 3, v & 3


def index(zl, c, x, y, zh):
    return (zl * 2 + c) * 64 + x * 16 + y * 4 + zh


def perm(move):
    return [(i, index(*move(*coords(i)))) for i in range(256)]


CORE = perm(lambda zl, c, x, y, zh: (zl, 1 - c, x, y, zh))
FIRST = {
    k: perm(lambda zl, c, x, y, zh, k=k: (zl, c, x ^ (k * (1 - c)), y ^ (k * c), zh))
    for k in (1, 2, 3)
}
SECOND = {
    k: perm(lambda zl, c, x, y, zh, k=k: (zl, c, x ^ (k * c), y ^ (k * (1 - c)), zh))
    for k in (1, 2, 3)
}


def send(value, pairs):
    return lax.ppermute(value, AXES, pairs)


def ring(value, perms):
    got = {k: send(value, perms[k]) for k in (1, 3, 2)}
    return got[1], got[2], got[3]


def place():
    return tuple(lax.axis_index(a) for a in AXES)


def block_at(c, x, y, first, second):
    in_x = jnp.where(c == 0, first, second)
    in_y = jnp.where(c == 0, second, first)
    return (x ^ in_x) * 4 + (y ^ in_y)


def dot(a, b, dims):
    return lax.dot_general(a, b, (dims, ((), ())), preferred_element_type=F32)


def window(at):
    start = pl.multiple_of(((at * 5) >> 1) * 128, 128)
    return pl.ds(start, WIDE), pl.multiple_of((at & 1) * 64, 64)


def spread_kernel(mine, out):
    for i in range(8):
        out[i] = mine[...]


def weave_kernel(along, out):
    for zh in range(4):
        for zl in range(2):
            tokens = slice(zl * 128, (zl + 1) * 128)
            out[zh * 80 : (zh + 1) * 80, tokens] = along[zl * 4 + zh, 0:80]
            out[NS + zh * 64 : NS + (zh + 1) * 64, tokens] = along[zl * 4 + zh, 80:144]


def near_kernel(t0, t1, t3, ws, wso, wt, wto, s_ref, t_ref, hs, ht):
    _, c, x, y, _ = place()
    for j, t in ((0, t0), (1, t1), (3, t3), (2, None)):
        for i in range(4):
            at = block_at(c, x, y, i, j)
            rows_s = pl.ds(pl.multiple_of(at * NS, NS), NS)
            rows_t = pl.ds(pl.multiple_of(at * NT, NT), NT)
            if t is None:
                hs[rows_s] = jnp.zeros((NS, TOK), BF16)
                ht[rows_t] = jnp.zeros((NT, TOK), BF16)
            else:
                hs[rows_s] = t[i, 0:NS]
                ht[rows_t] = t[i, NS : NS + NT]
    t_ref[:ROWS] = dot(wt[...], ht[...], ((1,), (0,)))
    t_ref[ROWS:] = dot(wto[...], ht[...], ((1,), (0,)))
    s_ref[:ROWS] = dot(ws[...], hs[...], ((1,), (0,)))
    s_ref[ROWS:] = dot(wso[...], hs[...], ((1,), (0,)))


def far_kernel(
    t2a, t2b, s_in, t_in, hs_in, ws, wso, wt, wto, es_ref, et_ref, st_ref, hs, pads
):
    _, c, x, y, _ = place()
    s_ref, t_ref = es_ref, et_ref
    hs[...] = hs_in[...]
    s_ref[...] = s_in[...]
    t_ref[...] = t_in[...]
    for i in range(4):
        line = t2a[i] if i < 2 else t2b[i - 2]
        at = block_at(c, x, y, i, 2)
        hs[pl.ds(pl.multiple_of(at * NS, NS), NS)] = line[0:NS]
        cols, first = window(at)
        pads[i] = jnp.zeros((WIDE, TOK), BF16)
        pads[i, pl.ds(first, NS)] = line[0:NS]
        cols_t = pl.ds(pl.multiple_of(at * NT, NT), NT)
        s_ref[:ROWS] += dot(ws[:, cols], pads[i], ((1,), (0,)))
        s_ref[ROWS:] += dot(wso[:, cols], pads[i], ((1,), (0,)))
        t_ref[:ROWS] += dot(wt[:, cols_t], line[NS:], ((1,), (0,)))
        t_ref[ROWS:] += dot(wto[:, cols_t], line[NS:], ((1,), (0,)))
    s, t = s_ref[...], t_ref[...]
    sm = jnp.max(s, axis=0, keepdims=True)
    tm = jnp.max(t, axis=0, keepdims=True)
    es, et = jnp.exp(s - sm), jnp.exp(t - tm)
    st_ref[0, 0:1] = sm
    st_ref[0, 1:2] = tm
    st_ref[0, 2:3] = jnp.sum(es, axis=0, keepdims=True)
    st_ref[0, 3:4] = jnp.sum(et, axis=0, keepdims=True)
    st_ref[0, 4:5] = jnp.sum(et * (t - s), axis=0, keepdims=True)
    st_ref[0, 5:8] = jnp.zeros((3, TOK), F32)
    for i in range(1, 8):
        st_ref[i] = st_ref[0]
    es_ref[...] = es
    et_ref[...] = et


def vmem_call(kernel, name, outs, scratch, flops, *args):
    vmem = pl.BlockSpec(memory_space=pltpu.VMEM)
    return pl.pallas_call(
        kernel,
        out_shape=tuple(jax.ShapeDtypeStruct(*o) for o in outs),
        in_specs=[vmem] * len(args),
        out_specs=(vmem,) * len(outs),
        scratch_shapes=[pltpu.VMEM(*o) for o in scratch],
        compiler_params=pltpu.CompilerParams(vmem_limit_bytes=VMEM_LIMIT),
        cost_estimate=pl.CostEstimate(flops=flops, bytes_accessed=14_000_000, transcendentals=0),
        name=name,
    )(*args)


LOGITS = ((2 * ROWS, TOK), F32)
HIDDEN = ((DS, TOK), BF16)


def near_call(t0, t1, t3, *weights):
    flops = 2 * 2 * ROWS * TOK * (DS + DT)
    outs = (LOGITS, LOGITS, HIDDEN)
    return vmem_call(near_kernel, "near", outs, [((DT, TOK), BF16)], flops, t0, t1, t3, *weights)


def far_call(*args):
    flops = 2 * 2 * ROWS * TOK * (DS + DT) // 3
    outs = (LOGITS, LOGITS, ((8, 8, TOK), F32), HIDDEN)
    return vmem_call(far_kernel, "far", outs, [((4, WIDE, TOK), BF16)], flops, *args)


def merged(stats, n):
    top = stats[0, 0:2]
    for i in range(1, n):
        top = jnp.maximum(top, stats[i, 0:2])
    totals, cross = jnp.zeros((2, TOK), F32), jnp.zeros((1, TOK), F32)
    for i in range(n):
        scale = jnp.exp(stats[i, 0:2] - top)
        totals += stats[i, 2:4] * scale
        cross += stats[i, 4:5] * scale[1:2]
    return top, totals, cross


def merge_kernel(stats, out):
    out[0, 0:2], out[0, 2:4], out[0, 4:5] = merged(stats, 8)
    out[0, 5:8] = jnp.zeros((3, TOK), F32)
    for i in range(1, 16):
        out[i] = out[0]


CHUNK = 1280


def opposite_kernel(
    stats, local, weights, es_ref, et_ref, ws, wso, kl_ref, g_own, g_oth, o2, part
):
    zl, c, x, y, _ = place()
    top, totals, cross = merged(stats, 16)
    kl = cross / totals[1:2] - top[1:2] - jnp.log(totals[1:2]) + top[0:1] + jnp.log(totals[0:1])
    kl_ref[...] = jnp.where(zl == 0, kl[:, :128], kl[:, 128:])
    weight = jnp.concatenate(
        [jnp.where(c == 0, weights[i : i + 1], weights[i + 1 : i + 2]) for i in (0, 2)], axis=1
    )
    coef = weight * (jnp.exp(local[0, 0:2] - top) / totals)
    g = (es_ref[...] * coef[0:1] - et_ref[...] * coef[1:2]).astype(BF16)
    g_own[...] = g[:ROWS]
    g_oth[...] = g[ROWS:]
    for r in range(4):
        cols, first = window(block_at(c, x, y, r, 2))
        whole = dot(g[:ROWS], ws[:, cols], ((0,), (0,))) + dot(g[ROWS:], wso[:, cols], ((0,), (0,)))
        part[r] = whole.astype(BF16).T
        o2[r] = part[r, pl.ds(first, NS)]


def rest_kernel(g_own, g_oth, ws, wso, o0, o1, o3, acc):
    _, c, x, y, _ = place()
    for n in range(DS // CHUNK):
        cols = slice(n * CHUNK, (n + 1) * CHUNK)
        part = dot(g_own[...], ws[:, cols], ((0,), (0,))) + dot(g_oth[...], wso[:, cols], ((0,), (0,)))
        acc[cols] = part.astype(BF16).T
    for k, o in ((0, o0), (1, o1), (3, o3)):
        for r in range(4):
            at = block_at(c, x, y, r, k)
            o[r] = acc[pl.ds(pl.multiple_of(at * NS, NS), NS)]


def opposite_call(*args):
    rows = ((ROWS, TOK), BF16)
    outs = (((1, 128), F32), rows, rows, ((4, NS, TOK), BF16))
    flops = 2 * 2 * ROWS * TOK * DS // 3
    return vmem_call(opposite_kernel, "opposite", outs, [((4, WIDE, TOK), BF16)], flops, *args)


def rest_call(*args):
    outs = (((4, NS, TOK), BF16),) * 3
    return vmem_call(rest_kernel, "rest", outs, [HIDDEN], 2 * 2 * ROWS * TOK * DS, *args)


def head_kernel(g_own, g_got, h_own, h_got, out):
    out[...] = (
        dot(g_own[...], h_own[...], ((1,), (1,))) + dot(g_got[...], h_got[...], ((1,), (1,)))
    ).astype(BF16)


def head_call(g_own, g_got, h_own, h_got):
    step = 640
    whole = pl.BlockSpec((ROWS, TOK), lambda i: (0, 0))
    some = pl.BlockSpec((step, TOK), lambda i: (i, 0))
    return pl.pallas_call(
        head_kernel,
        out_shape=jax.ShapeDtypeStruct((ROWS, DS), BF16),
        grid=(DS // step,),
        in_specs=[whole, whole, some, some],
        out_specs=pl.BlockSpec((ROWS, step), lambda i: (0, i)),
        compiler_params=pltpu.CompilerParams(vmem_limit_bytes=VMEM_LIMIT),
        cost_estimate=pl.CostEstimate(
            flops=2 * 2 * ROWS * TOK * DS, bytes_accessed=10_000_000, transcendentals=0
        ),
        name="head",
    )(g_own, g_got, h_own, h_got)


def per_device(student_hidden, teacher_hidden, student_head, teacher_head, row_weight):
    teacher_other = send(teacher_head, CORE)
    student_other = send(student_head, CORE)

    mine = jnp.concatenate([student_hidden.T, teacher_hidden.T], axis=0)
    copies = vmem_call(spread_kernel, "spread", [((8, 144, 128), BF16)], [], 1, mine)[0]
    along = lax.all_to_all(copies, ("zl", "zh"), 0, 0)
    block = vmem_call(weave_kernel, "weave", [((NS + NT, TOK), BF16)], [], 1, along)[0]
    line = jnp.stack((block,) + ring(block, FIRST))
    before, after = send(line, SECOND[1]), send(line, SECOND[3])
    far_low, far_high = send(after[:2], SECOND[1]), send(before[2:], SECOND[3])

    heads = (student_head, student_other, teacher_head, teacher_other)
    near = near_call(line, before, after, *heads)
    es, et, local, hidden_own = far_call(far_low, far_high, *near, *heads)
    stats = lax.all_to_all(local, ("zl", "zh"), 0, 0)
    stats = vmem_call(merge_kernel, "merge", [((16, 8, TOK), F32)], [], 1, stats)[0]
    stats = lax.all_to_all(stats, ("x", "y"), 0, 0)
    kl_rows, g_own, g_oth, o2 = opposite_call(
        stats, local, row_weight.reshape(4, 128), es, et, student_head, student_other
    )
    r2 = send(o2, SECOND[2])
    g_got, hidden_got = send(g_oth, CORE), send(hidden_own, CORE)
    g_got, hidden_got, o0, o1, o3 = lax.optimization_barrier(
        (g_got, hidden_got, *rest_call(g_own, g_oth, student_head, student_other))
    )
    r1, r3 = send(o1, SECOND[1]), send(o3, SECOND[3])
    head_grad = head_call(g_own, g_got, hidden_own, hidden_got)
    r1, r2, r3, head_grad = lax.optimization_barrier((r1, r2, r3, head_grad))

    sums = o0.astype(F32) + (r1.astype(F32) + r3.astype(F32)) + r2.astype(F32)
    r1, r3, r2 = (send(sums[k].astype(BF16), FIRST[k]) for k in (1, 3, 2))
    sums = sums[0] + (r1.astype(F32) + r3.astype(F32)) + r2.astype(F32)
    sums = jnp.concatenate([sums[:, :128], sums[:, 128:]], axis=0).reshape(8, 80, 128)
    hidden_grad = jnp.sum(lax.all_to_all(sums, ("zl", "zh"), 0, 0), axis=0).T
    return (kl_rows.reshape(128), hidden_grad, head_grad)


def solution(mesh):
    fine = jax.sharding.Mesh(mesh.devices.reshape(2, 2, 4, 4, 4), AXES)
    pipe, vocab = AXES[:2], AXES[2:]
    placed = (P(pipe, vocab), P(pipe, vocab), P(AXES, None), P(AXES, None), P())
    return jax.shard_map(
        per_device,
        mesh=fine,
        in_specs=placed,
        out_specs=(P(pipe), P(pipe, vocab), P(AXES, None)),
        check_vma=False,
    )
```

```python
import jax
import jax.numpy as jnp
from jax import lax
from jax.experimental import pallas as pl
from jax.experimental.pallas import tpu as pltpu
from jax.sharding import PartitionSpec as P

DS, DT = 5120, 4096
ROWS = 384
TOK = 256
NS, NT = 320, 256
WIDE = 384
AXES = ("zl", "c", "x", "y", "zh")
F32, BF16 = jnp.float32, jnp.bfloat16
VMEM_LIMIT = 20 * 1024 * 1024


def coords(i):
    p, v = divmod(i, 64)
    return p >> 1, p & 1, v >> 4, (v >> 2) & 3, v & 3


def index(zl, c, x, y, zh):
    return (zl * 2 + c) * 64 + x * 16 + y * 4 + zh


def perm(move):
    return [(i, index(*move(*coords(i)))) for i in range(256)]


CORE = perm(lambda zl, c, x, y, zh: (zl, 1 - c, x, y, zh))
FIRST = {
    k: perm(lambda zl, c, x, y, zh, k=k: (zl, c, x ^ (k * (1 - c)), y ^ (k * c), zh))
    for k in (1, 2, 3)
}
SECOND = {
    k: perm(lambda zl, c, x, y, zh, k=k: (zl, c, x ^ (k * c), y ^ (k * (1 - c)), zh))
    for k in (1, 2, 3)
}


def send(value, pairs):
    return lax.ppermute(value, AXES, pairs)


def ring(value, perms):
    got = {k: send(value, perms[k]) for k in (1, 3, 2)}
    return got[1], got[2], got[3]


def place():
    return tuple(lax.axis_index(a) for a in AXES)


def block_at(c, x, y, first, second):
    in_x = jnp.where(c == 0, first, second)
    in_y = jnp.where(c == 0, second, first)
    return (x ^ in_x) * 4 + (y ^ in_y)


def dot(a, b, dims):
    return lax.dot_general(a, b, (dims, ((), ())), preferred_element_type=F32)


def window(at):
    start = pl.multiple_of(((at * 5) >> 1) * 128, 128)
    return pl.ds(start, WIDE), pl.multiple_of((at & 1) * 64, 64)


def spread_kernel(mine, out):
    for i in range(8):
        out[i] = mine[...]


def weave_kernel(along, out):
    for zh in range(4):
        for zl in range(2):
            tokens = slice(zl * 128, (zl + 1) * 128)
            out[zh * 80 : (zh + 1) * 80, tokens] = along[zl * 4 + zh, 0:80]
            out[NS + zh * 64 : NS + (zh + 1) * 64, tokens] = along[zl * 4 + zh, 80:144]


def near_kernel(t0, t1, t3, ws, wso, wt, wto, s_ref, t_ref, hs, ht):
    _, c, x, y, _ = place()
    for j, t in ((0, t0), (1, t1), (3, t3), (2, None)):
        for i in range(4):
            at = block_at(c, x, y, i, j)
            rows_s = pl.ds(pl.multiple_of(at * NS, NS), NS)
            rows_t = pl.ds(pl.multiple_of(at * NT, NT), NT)
            if t is None:
                hs[rows_s] = jnp.zeros((NS, TOK), BF16)
                ht[rows_t] = jnp.zeros((NT, TOK), BF16)
            else:
                hs[rows_s] = t[i, 0:NS]
                ht[rows_t] = t[i, NS : NS + NT]
    t_ref[:ROWS] = dot(wt[...], ht[...], ((1,), (0,)))
    t_ref[ROWS:] = dot(wto[...], ht[...], ((1,), (0,)))
    s_ref[:ROWS] = dot(ws[...], hs[...], ((1,), (0,)))
    s_ref[ROWS:] = dot(wso[...], hs[...], ((1,), (0,)))


def far_kernel(
    t2a, t2b, s_in, t_in, hs_in, ws, wso, wt, wto, es_ref, et_ref, st_ref, hs, pads
):
    _, c, x, y, _ = place()
    s_ref, t_ref = es_ref, et_ref
    hs[...] = hs_in[...]
    s_ref[...] = s_in[...]
    t_ref[...] = t_in[...]
    for i in range(4):
        line = t2a[i] if i < 2 else t2b[i - 2]
        at = block_at(c, x, y, i, 2)
        hs[pl.ds(pl.multiple_of(at * NS, NS), NS)] = line[0:NS]
        cols, first = window(at)
        pads[i] = jnp.zeros((WIDE, TOK), BF16)
        pads[i, pl.ds(first, NS)] = line[0:NS]
        cols_t = pl.ds(pl.multiple_of(at * NT, NT), NT)
        s_ref[:ROWS] += dot(ws[:, cols], pads[i], ((1,), (0,)))
        s_ref[ROWS:] += dot(wso[:, cols], pads[i], ((1,), (0,)))
        t_ref[:ROWS] += dot(wt[:, cols_t], line[NS:], ((1,), (0,)))
        t_ref[ROWS:] += dot(wto[:, cols_t], line[NS:], ((1,), (0,)))
    s, t = s_ref[...], t_ref[...]
    sm = jnp.max(s, axis=0, keepdims=True)
    tm = jnp.max(t, axis=0, keepdims=True)
    es, et = jnp.exp(s - sm), jnp.exp(t - tm)
    st_ref[0, 0:1] = sm
    st_ref[0, 1:2] = tm
    st_ref[0, 2:3] = jnp.sum(es, axis=0, keepdims=True)
    st_ref[0, 3:4] = jnp.sum(et, axis=0, keepdims=True)
    st_ref[0, 4:5] = jnp.sum(et * (t - s), axis=0, keepdims=True)
    st_ref[0, 5:8] = jnp.zeros((3, TOK), F32)
    for i in range(1, 8):
        st_ref[i] = st_ref[0]
    es_ref[...] = es
    et_ref[...] = et


def vmem_call(kernel, name, outs, scratch, flops, *args):
    vmem = pl.BlockSpec(memory_space=pltpu.VMEM)
    return pl.pallas_call(
        kernel,
        out_shape=tuple(jax.ShapeDtypeStruct(*o) for o in outs),
        in_specs=[vmem] * len(args),
        out_specs=(vmem,) * len(outs),
        scratch_shapes=[pltpu.VMEM(*o) for o in scratch],
        compiler_params=pltpu.CompilerParams(vmem_limit_bytes=VMEM_LIMIT),
        cost_estimate=pl.CostEstimate(flops=flops, bytes_accessed=14_000_000, transcendentals=0),
        name=name,
    )(*args)


LOGITS = ((2 * ROWS, TOK), F32)
HIDDEN = ((DS, TOK), BF16)


def near_call(t0, t1, t3, *weights):
    flops = 2 * 2 * ROWS * TOK * (DS + DT)
    outs = (LOGITS, LOGITS, HIDDEN)
    return vmem_call(near_kernel, "near", outs, [((DT, TOK), BF16)], flops, t0, t1, t3, *weights)


def far_call(*args):
    flops = 2 * 2 * ROWS * TOK * (DS + DT) // 3
    outs = (LOGITS, LOGITS, ((8, 8, TOK), F32), HIDDEN)
    return vmem_call(far_kernel, "far", outs, [((4, WIDE, TOK), BF16)], flops, *args)


def merged(stats, n):
    top = stats[0, 0:2]
    for i in range(1, n):
        top = jnp.maximum(top, stats[i, 0:2])
    totals, cross = jnp.zeros((2, TOK), F32), jnp.zeros((1, TOK), F32)
    for i in range(n):
        scale = jnp.exp(stats[i, 0:2] - top)
        totals += stats[i, 2:4] * scale
        cross += stats[i, 4:5] * scale[1:2]
    return top, totals, cross


def merge_kernel(stats, out):
    out[0, 0:2], out[0, 2:4], out[0, 4:5] = merged(stats, 8)
    out[0, 5:8] = jnp.zeros((3, TOK), F32)
    for i in range(1, 16):
        out[i] = out[0]


CHUNK = 1280


def opposite_kernel(
    stats, local, weights, es_ref, et_ref, ws, wso, kl_ref, g_own, g_oth, o2, part
):
    zl, c, x, y, _ = place()
    top, totals, cross = merged(stats, 16)
    kl = cross / totals[1:2] - top[1:2] - jnp.log(totals[1:2]) + top[0:1] + jnp.log(totals[0:1])
    kl_ref[...] = jnp.where(zl == 0, kl[:, :128], kl[:, 128:])
    weight = jnp.concatenate(
        [jnp.where(c == 0, weights[i : i + 1], weights[i + 1 : i + 2]) for i in (0, 2)], axis=1
    )
    coef = weight * (jnp.exp(local[0, 0:2] - top) / totals)
    g = (es_ref[...] * coef[0:1] - et_ref[...] * coef[1:2]).astype(BF16)
    g_own[...] = g[:ROWS]
    g_oth[...] = g[ROWS:]
    for r in range(4):
        cols, first = window(block_at(c, x, y, r, 2))
        whole = dot(g[:ROWS], ws[:, cols], ((0,), (0,))) + dot(g[ROWS:], wso[:, cols], ((0,), (0,)))
        part[r] = whole.astype(BF16).T
        o2[r] = part[r, pl.ds(first, NS)]


def rest_kernel(g_own, g_oth, ws, wso, o0, o1, o3, acc):
    _, c, x, y, _ = place()
    for n in range(DS // CHUNK):
        cols = slice(n * CHUNK, (n + 1) * CHUNK)
        part = dot(g_own[...], ws[:, cols], ((0,), (0,))) + dot(g_oth[...], wso[:, cols], ((0,), (0,)))
        acc[cols] = part.astype(BF16).T
    for k, o in ((0, o0), (1, o1), (3, o3)):
        for r in range(4):
            at = block_at(c, x, y, r, k)
            o[r] = acc[pl.ds(pl.multiple_of(at * NS, NS), NS)]


def opposite_call(*args):
    rows = ((ROWS, TOK), BF16)
    outs = (((1, 128), F32), rows, rows, ((4, NS, TOK), BF16))
    flops = 2 * 2 * ROWS * TOK * DS // 3
    return vmem_call(opposite_kernel, "opposite", outs, [((4, WIDE, TOK), BF16)], flops, *args)


def rest_call(*args):
    outs = (((4, NS, TOK), BF16),) * 3
    return vmem_call(rest_kernel, "rest", outs, [HIDDEN], 2 * 2 * ROWS * TOK * DS, *args)


def head_kernel(g_own, g_got, h_own, h_got, out):
    out[...] = (
        dot(g_own[...], h_own[...], ((1,), (1,))) + dot(g_got[...], h_got[...], ((1,), (1,)))
    ).astype(BF16)


def head_call(g_own, g_got, h_own, h_got):
    step = 640
    whole = pl.BlockSpec((ROWS, TOK), lambda i: (0, 0))
    some = pl.BlockSpec((step, TOK), lambda i: (i, 0))
    return pl.pallas_call(
        head_kernel,
        out_shape=jax.ShapeDtypeStruct((ROWS, DS), BF16),
        grid=(DS // step,),
        in_specs=[whole, whole, some, some],
        out_specs=pl.BlockSpec((ROWS, step), lambda i: (0, i)),
        compiler_params=pltpu.CompilerParams(vmem_limit_bytes=VMEM_LIMIT),
        cost_estimate=pl.CostEstimate(
            flops=2 * 2 * ROWS * TOK * DS, bytes_accessed=10_000_000, transcendentals=0
        ),
        name="head",
    )(g_own, g_got, h_own, h_got)


def per_device(student_hidden, teacher_hidden, student_head, teacher_head, row_weight):
    teacher_other = send(teacher_head, CORE)
    student_other = send(student_head, CORE)

    mine = jnp.concatenate([student_hidden.T, teacher_hidden.T], axis=0)
    copies = vmem_call(spread_kernel, "spread", [((8, 144, 128), BF16)], [], 1, mine)[0]
    along = lax.all_to_all(copies, ("zl", "zh"), 0, 0)
    block = vmem_call(weave_kernel, "weave", [((NS + NT, TOK), BF16)], [], 1, along)[0]
    line = jnp.stack((block,) + ring(block, FIRST))
    before, after = send(line, SECOND[1]), send(line, SECOND[3])
    far_low, far_high = send(after[:2], SECOND[1]), send(before[2:], SECOND[3])

    heads = (student_head, student_other, teacher_head, teacher_other)
    near = near_call(line, before, after, *heads)
    es, et, local, hidden_own = far_call(far_low, far_high, *near, *heads)
    stats = lax.all_to_all(local, ("zl", "zh"), 0, 0)
    stats = vmem_call(merge_kernel, "merge", [((16, 8, TOK), F32)], [], 1, stats)[0]
    stats = lax.all_to_all(stats, ("x", "y"), 0, 0)
    kl_rows, g_own, g_oth, o2 = opposite_call(
        stats, local, row_weight.reshape(4, 128), es, et, student_head, student_other
    )
    r2 = send(o2, SECOND[2])
    g_got, hidden_got = send(g_oth, CORE), send(hidden_own, CORE)
    g_got, hidden_got, o0, o1, o3 = lax.optimization_barrier(
        (g_got, hidden_got, *rest_call(g_own, g_oth, student_head, student_other))
    )
    r1, r3 = send(o1, SECOND[1]), send(o3, SECOND[3])
    head_grad = head_call(g_own, g_got, hidden_own, hidden_got)
    r1, r2, r3, head_grad = lax.optimization_barrier((r1, r2, r3, head_grad))

    sums = o0.astype(F32) + (r1.astype(F32) + r3.astype(F32)) + r2.astype(F32)
    r1, r3, r2 = (send(sums[k].astype(BF16), FIRST[k]) for k in (1, 3, 2))
    sums = sums[0] + (r1.astype(F32) + r3.astype(F32)) + r2.astype(F32)
    sums = jnp.concatenate([sums[:, :128], sums[:, 128:]], axis=0).reshape(8, 80, 128)
    pieces = lax.all_to_all(sums.astype(BF16), ("zl", "zh"), 0, 0)
    hidden_grad = jnp.sum(pieces.astype(F32), axis=0).T
    return (kl_rows.reshape(128), hidden_grad, head_grad)


def solution(mesh):
    fine = jax.sharding.Mesh(mesh.devices.reshape(2, 2, 4, 4, 4), AXES)
    pipe, vocab = AXES[:2], AXES[2:]
    placed = (P(pipe, vocab), P(pipe, vocab), P(AXES, None), P(AXES, None), P())
    return jax.shard_map(
        per_device,
        mesh=fine,
        in_specs=placed,
        out_specs=(P(pipe), P(pipe, vocab), P(AXES, None)),
        check_vma=False,
    )
```
